128 devices in a mesh: dp: 16 (over z, x), mp: 8 (over y, core).
Axes of the slice: x: 4, y: 4, z: 4, core: 2. Of those that a mesh axis runs over, the one named last changes fastest.
Arguments:
- gradient: bfloat16 [16, 768, 8, 768], P(None, 'dp', None, 'mp'), may hold values from -1.5 to 1.5
- owner: int32 [128], replicated, may hold values from 0 to 127, as said below
- left_stat: float32 [16, 8, 2, 768, 768], P('dp', 'mp'), may hold values from -2 to 10, as said below
- right_stat: float32 [16, 8, 2, 768, 768], P('dp', 'mp'), may hold values from -2 to 10, as said below
- left_root: bfloat16 [16, 8, 2, 768, 768], P('dp', 'mp'), may hold values from -1 to 2, as said below
- right_root: bfloat16 [16, 8, 2, 768, 768], P('dp', 'mp'), may hold values from -1 to 2, as said below
Outputs:
- precond: bfloat16 [16, 768, 8, 768], P(None, 'dp', None, 'mp')
- left_new: float32 [16, 8, 2, 768, 768], P('dp', 'mp')
- right_new: float32 [16, 8, 2, 768, 768], P('dp', 'mp')
The draws below stay inside these ranges and needn't reach their ends.
Inputs may be any that keep to these rules, and one draw needn't show every extreme that they name: No owner is named by more than 2 blocks, and one owner is named by exactly 2. `left_stat`: Symmetric. `right_stat`: Symmetric. `left_root`: Symmetric. `right_root`: Symmetric.
All inputs are finite; a program needn't handle non-finite values.
Results may differ from the reference program's by a relative error of at most 0.0049.
Values may be sent and summed in bfloat16 or wider, within the bound.
No kernel may reach another device: no remote copies, remote signals or barrier semaphores. Data moves between devices by JAX's collectives and lax.ppermute only.
A program may use at most 128 MiB of HBM per device.

```python
import jax
import jax.numpy as jnp
from jax import lax

BLK = 768
NBR = 16
NBC = 8
OWNERS = 128
CAP = 2
N_DP = 16
N_MP = 8


def symmetric(key, level_lo, level_hi, spread, ratio):
    shape = (N_DP, N_MP, CAP, BLK, BLK)
    key_noise, key_level, key_scale = jax.random.split(key, 3)
    noise = jax.random.normal(key_noise, shape, jnp.float32) * spread
    noise = 0.5 * (noise + jnp.swapaxes(noise, 3, 4))
    level = jax.random.uniform(key_level, shape[:4], jnp.float32, level_lo, level_hi)
    eye = jnp.eye(BLK, dtype=jnp.float32)
    matrix = noise + level[..., None] * eye
    expo = jax.random.uniform(key_scale, shape[:4], jnp.float32, -0.5, 0.5)
    scales = jnp.exp(expo * jnp.log(ratio))
    return matrix * scales[..., :, None] * scales[..., None, :]


def draw_owner(key, part):
    key = jax.random.fold_in(key, 7)
    key_heavy, key_order, key_spread = jax.random.split(key, 3)
    count = NBR * NBC
    heavy = jax.random.randint(key_heavy, (), 0, OWNERS)
    order = jax.random.permutation(key_order, count)
    offsets = jax.random.permutation(key_spread, OWNERS - 1)
    others = (heavy + 1 + offsets[jnp.maximum(order - CAP, 0) % (OWNERS - 1)]) % OWNERS
    return jnp.where(order < CAP, heavy, others).astype(jnp.int32)


def draw_left_stat(key, part):
    key = jax.random.fold_in(key, 3)
    return symmetric(key, 0.5, 2.0, 0.05, 1.0)


def draw_right_stat(key, part):
    key = jax.random.fold_in(key, 5)
    return symmetric(key, 0.5, 2.0, 0.05, 1.0)


def draw_left_root(key, part):
    key = jax.random.fold_in(key, 9)
    return symmetric(key, 0.6, 1.4, 0.7 * BLK ** (-0.5), 1.0).astype(jnp.bfloat16)


def draw_right_root(key, part):
    key = jax.random.fold_in(key, 13)
    return symmetric(key, 0.6, 1.4, 0.7 * BLK ** (-0.5), 1.0).astype(jnp.bfloat16)


def steps_of(rng, extent, cuts, smallest, largest):
    loudness = 1.0
    for dim, parts in cuts:
        draws = jax.random.uniform(jax.random.fold_in(jax.random.fold_in(rng, 6), dim), (parts,), jnp.float32, smallest / len(cuts), largest / len(cuts))
        loudness = loudness * jnp.repeat(jnp.exp(draws), extent[dim] // parts).reshape((-1,) + (1,) * (len(extent) - 1 - dim))
    return loudness


def bell_draw(own_key, shape, width, reach, cuts=(), kind=jnp.bfloat16):
    values = jax.random.normal(own_key, shape, jnp.float32) * width
    if len(cuts) > 0:
        values = steps_of(own_key, shape, cuts, -0.22, 0.18) * values
    return jnp.clip(values, min=-reach, max=reach).astype(kind)


def setup_inputs(seed: int = 0) -> dict:
    streams_of = jax.random.split(jax.random.key(seed), 7)
    gradient = bell_draw(streams_of[0], (NBR, BLK, NBC, BLK), 0.25, 1.5, ((1, 16), (3, 8)))
    owner = draw_owner(jax.random.fold_in(streams_of[6], 71), 0)
    left_stat = draw_left_stat(jax.random.fold_in(streams_of[6], 71), 0)
    right_stat = draw_right_stat(jax.random.fold_in(streams_of[6], 71), 0)
    left_root = draw_left_root(jax.random.fold_in(streams_of[6], 71), 0)
    right_root = draw_right_root(jax.random.fold_in(streams_of[6], 71), 0)
    return dict(gradient=gradient, owner=owner, left_stat=left_stat, right_stat=right_stat, left_root=left_root, right_root=right_root)


stat_decay = 0.98


def reference(gradient, owner, left_stat, right_stat, left_root, right_root):
    row_blocks = gradient.shape[0]
    col_blocks = gradient.shape[2]
    count = row_blocks * col_blocks
    blocks = jnp.transpose(gradient, (0, 2, 1, 3)).reshape(count, BLK, BLK)
    positions = jnp.arange(count, dtype=jnp.int32)
    earlier = (owner[None, :] == owner[:, None]) & (positions[None, :] < positions[:, None])
    rank = jnp.sum(earlier.astype(jnp.int32), axis=1).astype(jnp.int32)
    row_dev = (owner // N_MP).astype(jnp.int32)
    col_dev = (owner % N_MP).astype(jnp.int32)
    roots_left = left_root[row_dev, col_dev, rank]
    roots_right = right_root[row_dev, col_dev, rank]

    def precondition(items):
        block, root_left, root_right = items
        left = jnp.dot(block, block.T, preferred_element_type=jnp.float32)
        right = jnp.dot(block.T, block, preferred_element_type=jnp.float32)
        half = jnp.dot(root_left, block, preferred_element_type=jnp.float32).astype(jnp.bfloat16)
        result = jnp.dot(half, root_right, preferred_element_type=jnp.float32).astype(jnp.bfloat16)
        return left, right, result

    left_gram, right_gram, results = lax.map(precondition, (blocks, roots_left, roots_right))
    left_place = jnp.zeros_like(left_stat).at[row_dev, col_dev, rank].set(left_gram)
    right_place = jnp.zeros_like(right_stat).at[row_dev, col_dev, rank].set(right_gram)
    left_new = stat_decay * left_stat + (1.0 - stat_decay) * left_place
    right_new = stat_decay * right_stat + (1.0 - stat_decay) * right_place
    precond = jnp.transpose(results.reshape(row_blocks, col_blocks, BLK, BLK), (0, 2, 1, 3))
    return precond, left_new, right_new
```

```python
import jax
import jax.numpy as jnp
from jax import lax
from jax.experimental import pallas as pl
from jax.experimental.pallas import tpu as pltpu
from jax.sharding import PartitionSpec as P

STAT_DECAY = 0.98
LANES = 128
F32 = jnp.float32
BF16 = jnp.bfloat16
MIB = 1024 * 1024
FALLBACK = True
HBM = pltpu.HBM
FIRST_SPANS = (8, 4, 4)
SPANS = (8, 8)


def spread_matrix(part, groups):
    row = lax.broadcasted_iota(jnp.int32, (groups * LANES, groups * part), 0)
    col = lax.broadcasted_iota(jnp.int32, (groups * LANES, groups * part), 1)
    hit = (row // LANES == col // part) & (row % LANES == col % part)
    return jnp.where(hit, 1.0, 0.0).astype(BF16)


def count_slots(owner_ref, seen_ref, block):
    dest = owner_ref[block]
    slot = seen_ref[dest]
    seen_ref[dest] = slot + 1
    return dest, slot


def clear_counts(seen_ref, devices):
    def clear(i, carry):
        seen_ref[i] = 0
        return carry

    lax.fori_loop(0, devices, clear, 0)


def pack_kernel(owner_ref, grad_ref, out_ref, rows_ref, seen_ref):
    row_blocks, row_part, col_blocks, col_part = grad_ref.shape
    devices, slots = out_ref.shape[:2]
    clear_counts(seen_ref, devices)
    rows_ref[...] = jnp.zeros_like(rows_ref)

    def clear(i, carry):
        for s in range(slots):
            out_ref[i, s] = jnp.zeros((row_part, LANES), BF16)
        return carry

    lax.fori_loop(0, devices, clear, 0)

    def block_row(r, carry):
        rows_ref[:, :col_part] = grad_ref[r].astype(F32).reshape(row_part * col_blocks, col_part)
        for c in range(col_blocks):
            dest, slot = count_slots(owner_ref, seen_ref, r * col_blocks + c)
            tile = rows_ref[pl.ds(c, row_part, stride=col_blocks), :]
            out_ref[dest, slot] = tile.astype(BF16)
        return carry

    lax.fori_loop(0, row_blocks, block_row, 0)


def unpack_kernel(owner_ref, back_ref, out_ref, rows_ref, seen_ref):
    row_blocks, row_part, col_blocks, col_part = out_ref.shape
    devices = back_ref.shape[0]
    clear_counts(seen_ref, devices)

    def block_row(r, carry):
        for c in range(col_blocks):
            dest, slot = count_slots(owner_ref, seen_ref, r * col_blocks + c)
            rows_ref[pl.ds(c, row_part, stride=col_blocks), :] = back_ref[dest, slot].astype(F32)
        rows = rows_ref[:, :col_part].reshape(row_part, col_blocks, col_part)
        out_ref[r] = rows.astype(BF16)
        return carry

    lax.fori_loop(0, row_blocks, block_row, 0)


def pad_kernel(root_ref, out_ref):
    width = root_ref.shape[1]
    part = width // (out_ref.shape[1] // LANES)
    groups = LANES // (LANES - part)
    spread = spread_matrix(part, groups)
    wide, narrow = spread.shape
    for g in range(width // narrow):
        rows = jnp.dot(spread, root_ref[0, g * narrow : (g + 1) * narrow, :], preferred_element_type=F32).astype(BF16)
        for h in range(width // narrow):
            cell = lax.dot_general(
                rows[:, h * narrow : (h + 1) * narrow], spread, (((1,), (1,)), ((), ())), preferred_element_type=F32
            )
            out_ref[0, g * wide : (g + 1) * wide, h * wide : (h + 1) * wide] = cell.astype(BF16)


def gather_tiles(arr_ref, wide_ref):
    row_groups, col_groups, _, row_part, _ = arr_ref.shape
    for a in range(row_groups):
        for m in range(col_groups):
            wide_ref[a * row_part : (a + 1) * row_part, m * LANES : (m + 1) * LANES] = arr_ref[a, m, 0]


def precond_kernel(arr_ref, left_ref, right_ref, out_ref, wide_ref):
    row_groups, col_groups, _, row_part, _ = arr_ref.shape
    gather_tiles(arr_ref, wide_ref)
    step = 4 * row_part
    for i in range(row_groups // 4):
        half = jnp.dot(left_ref[0, i * step : (i + 1) * step, :], wide_ref[...], preferred_element_type=F32).astype(BF16)
        result = jnp.dot(half, right_ref[0], preferred_element_type=F32).astype(BF16)
        for k in range(4):
            for m in range(col_groups):
                out_ref[4 * i + k, m, 0] = result[k * row_part : (k + 1) * row_part, m * LANES : (m + 1) * LANES]


def gram_kernel(arr_ref, left_ref, right_ref, left_out, right_out, wide_ref, block_ref):
    width = block_ref.shape[0]
    part = width // arr_ref.shape[1]
    tile = left_ref.shape[1]
    step = pl.program_id(1)

    @pl.when(step == 0)
    def _():
        gather_tiles(arr_ref, wide_ref)
        spread = spread_matrix(part, LANES // (LANES - part))
        wide, narrow = spread.shape
        for g in range(width // narrow):
            cols = jnp.dot(wide_ref[:, g * wide : (g + 1) * wide], spread, preferred_element_type=F32)
            block_ref[:, g * narrow : (g + 1) * narrow] = cols.astype(BF16)

    for i in range(width // tile):

        @pl.when(step == i)
        def _(i=i):
            mine = slice(i * tile, (i + 1) * tile)
            left = lax.dot_general(
                block_ref[mine, :], block_ref[...], (((1,), (1,)), ((), ())), preferred_element_type=F32
            )
            left_out[0] = STAT_DECAY * left_ref[0] + (1.0 - STAT_DECAY) * left
            right = lax.dot_general(
                block_ref[:, mine], block_ref[...], (((0,), (0,)), ((), ())), preferred_element_type=F32
            )
            right_out[0] = STAT_DECAY * right_ref[0] + (1.0 - STAT_DECAY) * right


def general_path(gradient, owner, left_stat, right_stat, left_root, right_root):
    row_blocks, row_part, col_blocks, col_part = gradient.shape
    dp_count = lax.axis_size("dp")
    mp_count = lax.axis_size("mp")
    devices = dp_count * mp_count
    slots, width = left_stat.shape[2:4]
    wide = mp_count * LANES
    smem = pl.BlockSpec(memory_space=pltpu.SMEM)
    vmem = pl.BlockSpec(memory_space=pltpu.VMEM)
    rows_scratch = pltpu.VMEM((row_part * col_blocks, LANES), F32)
    seen_scratch = pltpu.SMEM((devices,), jnp.int32)

    def exchange(x):
        return lax.all_to_all(x, ("dp", "mp"), split_axis=0, concat_axis=0, tiled=True)

    outgoing = pl.pallas_call(
        pack_kernel,
        out_shape=jax.ShapeDtypeStruct((devices, slots, row_part, LANES), BF16),
        in_specs=[smem, vmem],
        out_specs=vmem,
        scratch_shapes=[rows_scratch, seen_scratch],
        compiler_params=pltpu.CompilerParams(vmem_limit_bytes=12 * MIB),
        name="pack",
    )(owner, gradient)
    padded_root = pl.pallas_call(
        pad_kernel,
        grid=(slots,),
        out_shape=jax.ShapeDtypeStruct((slots, wide, wide), BF16),
        in_specs=[pl.BlockSpec((1, width, width), lambda s: (s, 0, 0))],
        out_specs=pl.BlockSpec((1, wide, wide), lambda s: (s, 0, 0)),
        cost_estimate=pl.CostEstimate(flops=slots * 4 * 10**9, bytes_accessed=7 * 10**6, transcendentals=0),
        compiler_params=pltpu.CompilerParams(vmem_limit_bytes=24 * MIB),
        name="pad_right_root",
    )(right_root[0, 0])
    tiles = (dp_count, mp_count, slots, row_part, LANES)
    arrived = exchange(outgoing).reshape(tiles)
    tile_spec = pl.BlockSpec((dp_count, mp_count, 1, row_part, LANES), lambda s, *_: (0, 0, s, 0, 0))
    leaving = pl.pallas_call(
        precond_kernel,
        grid=(slots,),
        out_shape=jax.ShapeDtypeStruct(tiles, BF16),
        in_specs=[
            tile_spec,
            pl.BlockSpec((1, width, width), lambda s: (s, 0, 0)),
            pl.BlockSpec((1, wide, wide), lambda s: (s, 0, 0)),
        ],
        out_specs=tile_spec,
        scratch_shapes=[pltpu.VMEM((width, wide), BF16)],
        cost_estimate=pl.CostEstimate(flops=slots * 3 * 10**9, bytes_accessed=13 * 10**6, transcendentals=0),
        compiler_params=pltpu.CompilerParams(vmem_limit_bytes=30 * MIB),
        name="precondition",
    )(arrived, left_root[0, 0], padded_root)
    returned = exchange(leaving.reshape(outgoing.shape))
    tile = width // 3
    stat_spec = pl.BlockSpec((1, tile, width), lambda s, i: (s, i, 0))
    left_new, right_new = pl.pallas_call(
        gram_kernel,
        grid=(slots, width // tile),
        out_shape=[jax.ShapeDtypeStruct((slots, width, width), F32)] * 2,
        in_specs=[tile_spec, stat_spec, stat_spec],
        out_specs=[stat_spec, stat_spec],
        scratch_shapes=[pltpu.VMEM((width, wide), BF16), pltpu.VMEM((width, width), BF16)],
        cost_estimate=pl.CostEstimate(flops=slots * 3 * 10**9, bytes_accessed=22 * 10**6, transcendentals=0),
        compiler_params=pltpu.CompilerParams(vmem_limit_bytes=30 * MIB),
        name="grams",
    )(arrived, left_stat[0, 0], right_stat[0, 0])
    precond = pl.pallas_call(
        unpack_kernel,
        out_shape=jax.ShapeDtypeStruct(gradient.shape, BF16),
        in_specs=[smem, vmem],
        out_specs=vmem,
        scratch_shapes=[rows_scratch, seen_scratch],
        compiler_params=pltpu.CompilerParams(vmem_limit_bytes=12 * MIB),
        name="unpack",
    )(owner, returned)
    return (precond, left_new[None, None], right_new[None, None])


def copy_in(src, dst, sem):
    copy = pltpu.make_async_copy(src, dst, sem)
    copy.start()
    return copy


def lane_of(shape):
    return lax.broadcasted_iota(jnp.int32, shape, len(shape) - 1)


def pack_pairs_kernel(
    owner_hbm, grad_hbm, out_hbm, table_hbm, bad_hbm, owner_ref, grad_ref, out_ref, rows_ref, table_ref, bad_ref, seen_ref, first_ref,
    pairs_ref, load_sems, store_sems, sems,
):
    row_blocks, row_part, col_blocks, col_part = grad_ref.shape
    devices, height = out_hbm.shape[:2]
    count = row_blocks * col_blocks
    tall = row_part * col_blocks
    chunks = load_sems.shape[0]
    span = row_blocks // chunks
    owner_copy = copy_in(owner_hbm, owner_ref, sems.at[0])
    copies = []
    for i in range(chunks):
        part = pl.ds(i * span, span)
        copies.append(copy_in(grad_hbm.at[part], grad_ref.at[part], load_sems.at[i]))
    me = lax.axis_index("dp") * lax.axis_size("mp") + lax.axis_index("mp")
    half = col_part // 2
    free = LANES - col_part
    rest = half - free
    groups = row_part // 8
    extras_at = devices
    info_at = 2 * devices

    def clear(i, carry):
        seen_ref[i] = 0
        pairs_ref[i] = 0
        first_ref[i] = count
        return carry

    lax.fori_loop(0, devices, clear, 0, unroll=8)
    rows_ref[pl.ds(row_blocks * tall, tall), :] = jnp.zeros((tall, LANES), F32)
    owner_copy.wait()

    def block_row(r, extras):
        rows_ref[pl.ds(r * tall, tall), col_part:] = jnp.zeros((tall, free), F32)
        rows_ref[pl.ds(r * tall, tall), :col_part] = grad_ref[r].astype(F32).reshape(tall, col_part)
        for c in range(col_blocks):
            block = r * col_blocks + c
            dest, slot = count_slots(owner_ref, seen_ref, block)
            table_ref[block] = jnp.where(slot == 0, dest, 0)
            first_ref[jnp.where(slot == 0, dest, devices)] = block
            table_ref[extras_at + extras] = block
            extras = extras + slot
        return extras

    extras = jnp.int32(0)
    for i in range(chunks):
        copies[i].wait()
        extras = lax.fori_loop(i * span, (i + 1) * span, block_row, extras)
    for i in range(3):
        table_ref[info_at + i] = 0
    table_ref[info_at + 3] = extras
    bad_ref[0] = 0

    def note(e, carry):
        dest = owner_ref[table_ref[extras_at + e]]
        pairs = pairs_ref[dest // 2]
        pairs_ref[dest // 2] = pairs + 1
        here = dest // 2 == me // 2
        table_ref[info_at] = jnp.where(here, 1, table_ref[info_at])
        table_ref[info_at + 1] = jnp.where(here, dest % 2, table_ref[info_at + 1])
        table_ref[info_at + 2] = jnp.where(dest == me, 1, table_ref[info_at + 2])
        bad_ref[0] = jnp.where(pairs > 0, 1, bad_ref[0])
        return carry

    lax.fori_loop(0, extras, note, 0)
    table_copy = copy_in(table_ref, table_hbm, sems.at[1])
    bad_copy = copy_in(bad_ref, bad_hbm, sems.at[2])

    def tile_of(block):
        return rows_ref[pl.ds(block // col_blocks * tall + block % col_blocks, row_part, stride=col_blocks), :]

    def message(d, carry):
        tile = tile_of(first_ref[d])
        out_ref[d] = jnp.concatenate([tile, jnp.zeros((height - row_part, LANES), F32)], axis=0).astype(BF16)
        return carry

    stores = []
    share = devices // chunks
    for i in range(chunks):
        lax.fori_loop(i * share, (i + 1) * share, message, 0, unroll=8)

        def extra(e, carry, i=i):
            block = table_ref[extras_at + e]
            chip = owner_ref[block] // 2

            @pl.when(2 * chip // share == i)
            def _():
                tile = tile_of(block)
                lane = lane_of((row_part, LANES))
                lane8 = lane_of((8, LANES))
                for j in range(2):
                    old = out_ref[2 * chip + j].astype(F32)
                    moved = pltpu.roll(tile, (col_part - half * j) % LANES, 1)
                    top = jnp.where(lane < col_part, old[:row_part], moved)
                    low = jnp.zeros((8, LANES), F32)
                    for k in range(groups):
                        piece = pltpu.roll(tile[8 * k : 8 * k + 8], (rest * k - half * j - free) % LANES, 1)
                        low = jnp.where(lane8 // rest == k, piece, low)
                    out_ref[2 * chip + j] = jnp.concatenate([top, low], axis=0).astype(BF16)

            return carry

        lax.fori_loop(0, extras, extra, 0)
        part = pl.ds(i * share, share)
        stores.append(copy_in(out_ref.at[part], out_hbm.at[part], store_sems.at[i]))
    table_copy.wait()
    bad_copy.wait()
    for store in stores:
        store.wait()


def unpack_pairs_kernel(owner_hbm, table_hbm, back_ref, out_hbm, owner_ref, table_ref, out_ref, rows_ref, sems, store_sems):
    row_blocks, row_part, col_blocks, col_part = out_ref.shape
    devices = back_ref.shape[0]
    owner_copy = copy_in(owner_hbm, owner_ref, sems.at[0])
    table_copy = copy_in(table_hbm, table_ref, sems.at[1])
    half = col_part // 2
    free = LANES - col_part
    rest = half - free
    groups = row_part // 8
    chunks = store_sems.shape[0]
    span = row_blocks // chunks
    owner_copy.wait()
    table_copy.wait()

    def finish(r, buffer):
        rows = rows_ref[buffer, :, :col_part].reshape(row_part, col_blocks, col_part)
        out_ref[r] = rows.astype(BF16)

    def block_row(r, buffer):
        for c in range(col_blocks):
            tile = back_ref[table_ref[r * col_blocks + c], :row_part, :]
            rows_ref[buffer, pl.ds(c, row_part, stride=col_blocks), :] = tile.astype(F32)
        finish(r, buffer)

    def body(t, carry):
        block_row(2 * t, 0)
        block_row(2 * t + 1, 1)
        return carry

    stores = []
    for i in range(chunks):
        lax.fori_loop(i * span // 2, (i + 1) * span // 2, body, 0)

        def extra(e, carry, i=i):
            block = table_ref[devices + e]
            chip = owner_ref[block] // 2
            r = block // col_blocks

            @pl.when(r // span == i)
            def _():
                lane = lane_of((row_part, LANES))
                tile = jnp.zeros((row_part, LANES), F32)
                for j in range(2):
                    message = back_ref[2 * chip + j].astype(F32)
                    top = pltpu.roll(message[:row_part], (half * j - col_part) % LANES, 1)
                    low = [
                        pltpu.roll(message[row_part : row_part + 8], (half * j + free - rest * k) % LANES, 1)
                        for k in range(groups)
                    ]
                    low = jnp.concatenate(low, axis=0)
                    tile = jnp.where((lane >= half * j) & (lane < half * j + free), top, tile)
                    tile = jnp.where((lane >= half * j + free) & (lane < half * j + half), low, tile)
                rows_ref[0, :, :col_part] = out_ref[r].astype(F32).reshape(row_part * col_blocks, col_part)
                rows_ref[0, pl.ds(block % col_blocks, row_part, stride=col_blocks), :] = tile
                finish(r, 0)

            return carry

        lax.fori_loop(0, table_ref[2 * devices + 3], extra, 0)
        part = pl.ds(i * span, span)
        stores.append(copy_in(out_ref.at[part], out_hbm.at[part], store_sems.at[i]))
    for store in stores:
        store.wait()


def halves_order(shape, core, axis, part, groups):
    half = part // 2
    free = LANES - part
    rest = half - free
    n = lax.broadcasted_iota(jnp.int32, shape, axis)
    tail = n - free * groups
    first = part * (n // free) + n % free
    second = part * (tail // rest) + free + tail % rest
    return half * core + jnp.where(tail < 0, first, second)


def swap_groups(rows, rest):
    rows = list(rows)
    count = len(rows)
    group = lane_of(rows[0].shape) // rest
    bit = 1
    while bit < count:
        low = group // bit % 2 == 0
        for i in range(count):
            if i // bit % 2 == 0:
                x, y = rows[i], rows[i + bit]
                rows[i] = jnp.where(low, x, pltpu.roll(y, rest * bit, 1))
                rows[i + bit] = jnp.where(low, pltpu.roll(x, LANES - rest * bit, 1), y)
        bit *= 2
    return rows


def prepare_kernel(
    table_ref, left_hbm, right_hbm, left_other_hbm, right_other_hbm, padded_ref, picked_ref, left0_ref, left1_ref, root_ref, root1_ref,
    sems,
):
    width = root_ref.shape[0]
    groups = padded_ref.shape[0] // LANES
    part = width // groups
    half = width // 2
    core = lax.axis_index("mp") % 2
    info_at = table_ref.shape[0] - LANES
    left0_copy = copy_in(left_hbm.at[0], left0_ref, sems.at[0])
    root_copy = copy_in(right_hbm.at[0], root_ref, sems.at[1])
    from_other = (table_ref[info_at] == 1) & (table_ref[info_at + 1] != core)

    @pl.when(from_other)
    def _():
        right = copy_in(right_other_hbm.at[1], root1_ref, sems.at[2])
        copy_in(left_other_hbm.at[1], left1_ref, sems.at[3]).wait()
        right.wait()

    @pl.when(jnp.logical_not(from_other))
    def _():
        right = copy_in(right_hbm.at[1], root1_ref, sems.at[2])
        copy_in(left_hbm.at[1], left1_ref, sems.at[3]).wait()
        right.wait()

    mine = jnp.where(
        halves_order((width, half), core, 1, part, groups) == lax.broadcasted_iota(jnp.int32, (width, half), 0), 1.0, 0.0
    ).astype(BF16)
    cols = jnp.dot(root1_ref[...], mine, preferred_element_type=F32).astype(BF16)
    for j in range(2):
        theirs = jnp.where(
            halves_order((half, width), j, 0, part, groups) == lax.broadcasted_iota(jnp.int32, (half, width), 1), 1.0, 0.0
        ).astype(BF16)
        picked_ref[j * half : (j + 1) * half, :] = jnp.dot(theirs, cols, preferred_element_type=F32).astype(BF16)
    root_copy.wait()
    spread = spread_matrix(part, LANES // (LANES - part))
    wide, narrow = spread.shape
    for g in range(width // narrow):
        rows = jnp.dot(spread, root_ref[g * narrow : (g + 1) * narrow, :], preferred_element_type=F32).astype(BF16)
        for h in range(width // narrow):
            cell = lax.dot_general(
                rows[:, h * narrow : (h + 1) * narrow], spread, (((1,), (1,)), ((), ())), preferred_element_type=F32
            )
            padded_ref[g * wide : (g + 1) * wide, h * wide : (h + 1) * wide] = cell.astype(BF16)
    left0_copy.wait()


def take_matrix(part):
    free = LANES - part
    shape = ((LANES // free) * LANES, LANES)
    row = lax.broadcasted_iota(jnp.int32, shape, 0)
    col = lax.broadcasted_iota(jnp.int32, shape, 1)
    return jnp.where((row // LANES == col // free) & (row % LANES == part + col % free), 1.0, 0.0).astype(BF16)


def extract_kernel(arr_ref, roots_hbm, out_ref, tall_ref):
    row_groups, col_groups, height, _ = arr_ref.shape
    row_part = height - 8
    width = row_groups * row_part
    part = width // col_groups
    take = take_matrix(part)
    span = take.shape[0] // LANES
    for g in range(col_groups // span):
        tiles = [arr_ref[:, g * span + m, :row_part, :].reshape(width, LANES) for m in range(span)]
        cols = jnp.dot(jnp.concatenate(tiles, axis=1), take, preferred_element_type=F32)
        out_ref[:, g * LANES : (g + 1) * LANES] = cols.astype(BF16)
    low = [arr_ref[:, m, row_part:, :].astype(F32).reshape(8 * row_groups, LANES) for m in range(col_groups)]
    low = swap_groups(low, LANES // col_groups)
    for k in range(row_part // 8):
        tall_ref[:, k] = low[k].reshape(row_groups, 8, LANES)
    out_ref[:, width // 2 - LANES :] = tall_ref[...].reshape(width, LANES).astype(BF16)


def first_kernel(arr_ref, left_ref, right_ref, out_hbm, wide_ref, out_ref, out_sems):
    row_groups, col_groups, row_part, _ = out_ref.shape
    for a in range(row_groups):
        for m in range(col_groups):
            wide_ref[a * row_part : (a + 1) * row_part, m * LANES : (m + 1) * LANES] = arr_ref[a, m, :row_part, :]
    stores = []
    start = 0
    for i, span in enumerate(FIRST_SPANS):
        left = left_ref[start * row_part : (start + span) * row_part, :]
        half = jnp.dot(left, wide_ref[...], preferred_element_type=F32).astype(BF16)
        result = jnp.dot(half, right_ref[...], preferred_element_type=F32).astype(BF16)
        for k in range(span):
            for m in range(col_groups):
                out_ref[start + k, m] = result[k * row_part : (k + 1) * row_part, m * LANES : (m + 1) * LANES]
        rows = pl.ds(start, span)
        stores.append(copy_in(out_ref.at[rows], out_hbm.at[rows, :, pl.ds(0, row_part), :], out_sems.at[i]))
        start += span
    for store in stores:
        store.wait()


def extra_kernel(
    mine_ref, other_ref, left_ref, picked_ref, first_hbm, out_hbm, block_hbm, message_ref, block_ref, top_ref, load_sems,
    store_sems, block_sem,
):
    row_groups, col_groups, height, _ = message_ref.shape
    row_part = height - 8
    width = left_ref.shape[0]
    half = width // 2
    groups = row_part // 8
    core = lax.axis_index("mp") % 2
    loads = []
    start = 0
    for i, span in enumerate(SPANS):
        rows = pl.ds(start, span)
        loads.append(copy_in(first_hbm.at[rows], message_ref.at[rows], load_sems.at[i]))
        start += span
    for j in range(2):

        @pl.when(core == j)
        def _(j=j):
            block_ref[:, j * half : (j + 1) * half] = mine_ref[...]
            block_ref[:, (1 - j) * half : (2 - j) * half] = other_ref[...]

    block_copy = copy_in(block_ref, block_hbm, block_sem)
    take = take_matrix(width // col_groups)
    wide = take.shape[0]
    transposed = (((1,), (1,)), ((), ()))
    stores = []
    start = 0
    for i, span in enumerate(SPANS):
        left = left_ref[start * row_part : (start + span) * row_part, :]
        temp = jnp.dot(left, block_ref[...], preferred_element_type=F32).astype(BF16)
        result = jnp.dot(temp, picked_ref[...], preferred_element_type=F32)
        top = result[:, : half - LANES].astype(BF16)
        for g in range(col_groups * LANES // wide):
            spread = lax.dot_general(top[:, g * LANES : (g + 1) * LANES], take, transposed, preferred_element_type=F32)
            top_ref[: span * row_part, g * wide : (g + 1) * wide] = spread.astype(BF16)
        rows = result[:, half - LANES :].reshape(span, groups, 8, LANES)
        low = [rows[:, k].reshape(8 * span, LANES) for k in range(groups)]
        low += [jnp.zeros((8 * span, LANES), F32)] * (col_groups - groups)
        low = swap_groups(low, LANES // col_groups)
        loads[i].wait()
        for k in range(span):
            for m in range(col_groups):
                cols = slice(m * LANES, (m + 1) * LANES)
                message_ref[start + k, m, :row_part] += top_ref[k * row_part : (k + 1) * row_part, cols]
                message_ref[start + k, m, row_part:] = low[m][8 * k : 8 * k + 8].astype(BF16)
        rows = pl.ds(start, span)
        stores.append(copy_in(message_ref.at[rows], out_hbm.at[rows], store_sems.at[i]))
        start += span
    for store in stores:
        store.wait()
    block_copy.wait()


def pair_gram_kernel(table_ref, arr_ref, halves_ref, left_ref, right_ref, left_out, right_out, wide_ref, block_ref):
    width = block_ref.shape[0]
    row_groups, col_groups, height, _ = arr_ref.shape
    row_part = width // row_groups
    part = width // col_groups
    tile = left_ref.shape[1]
    slot = pl.program_id(0)
    step = pl.program_id(1)
    has_extra = table_ref[table_ref.shape[0] - LANES + 2]

    @pl.when((step == 0) & (slot == 0))
    def _():
        for a in range(row_groups):
            for m in range(col_groups):
                wide_ref[a * row_part : (a + 1) * row_part, m * LANES : (m + 1) * LANES] = arr_ref[a, m][:row_part]
        spread = spread_matrix(part, LANES // (LANES - part))
        wide, narrow = spread.shape
        for g in range(width // narrow):
            cols = jnp.dot(wide_ref[:, g * wide : (g + 1) * wide], spread, preferred_element_type=F32)
            block_ref[:, g * narrow : (g + 1) * narrow] = cols.astype(BF16)

    @pl.when((step == 0) & (slot == 1) & (has_extra == 1))
    def _():
        half = width // 2
        total = jnp.zeros((width, width), F32)
        for j in range(2):
            order = halves_order((half, width), j, 0, part, col_groups)
            theirs = jnp.where(order == lax.broadcasted_iota(jnp.int32, (half, width), 1), 1.0, 0.0).astype(BF16)
            total += jnp.dot(halves_ref[:, j * half : (j + 1) * half], theirs, preferred_element_type=F32)
        block_ref[...] = total.astype(BF16)

    @pl.when((step == 0) & (slot == 1) & (has_extra == 0))
    def _():
        block_ref[...] = jnp.zeros_like(block_ref)

    for i in range(width // tile):

        @pl.when(step == i)
        def _(i=i):
            mine = slice(i * tile, (i + 1) * tile)
            left = lax.dot_general(
                block_ref[mine, :], block_ref[...], (((1,), (1,)), ((), ())), preferred_element_type=F32
            )
            left_out[0] = STAT_DECAY * left_ref[0] + (1.0 - STAT_DECAY) * left
            right = lax.dot_general(
                block_ref[:, mine], block_ref[...], (((0,), (0,)), ((), ())), preferred_element_type=F32
            )
            right_out[0] = STAT_DECAY * right_ref[0] + (1.0 - STAT_DECAY) * right


def exchange(x):
    return lax.all_to_all(x, ("dp", "mp"), split_axis=0, concat_axis=0, tiled=True)


def other_core(x):
    count = lax.axis_size("mp")
    return lax.ppermute(x, "mp", [(i, i ^ 1) for i in range(count)])


def pair_path(outgoing, table, gradient, owner, left_stat, right_stat, left_root, right_root):
    row_blocks, row_part, col_blocks, col_part = gradient.shape
    dp_count = lax.axis_size("dp")
    mp_count = lax.axis_size("mp")
    devices = dp_count * mp_count
    slots, width = left_stat.shape[2:4]
    wide = mp_count * LANES
    height = outgoing.shape[1]
    groups = row_part // 8
    pieces = 4
    smem = pl.BlockSpec(memory_space=pltpu.SMEM)
    vmem = pl.BlockSpec(memory_space=pltpu.VMEM)
    hbm = pl.BlockSpec(memory_space=HBM)
    dma = pltpu.SemaphoreType.DMA
    message_shape = (dp_count, mp_count, height, LANES)
    left_root = left_root[0, 0]
    right_root = right_root[0, 0]

    def params(mib):
        return pltpu.CompilerParams(vmem_limit_bytes=mib * MIB)

    def cost(flops, moved):
        return pl.CostEstimate(flops=int(flops * 1e9), bytes_accessed=int(moved * 1e6), transcendentals=0)

    def in_hbm(x):
        return pltpu.with_memory_space_constraint(x, HBM)

    arrived = exchange(outgoing).reshape(message_shape)
    padded, picked, left0, left1 = pl.pallas_call(
        prepare_kernel,
        out_shape=[
            HBM((wide, wide), BF16),
            HBM((width, width // 2), BF16),
            HBM((width, width), BF16),
            HBM((width, width), BF16),
        ],
        in_specs=[smem, hbm, hbm, hbm, hbm],
        out_specs=[vmem] * 4,
        scratch_shapes=[pltpu.VMEM((width, width), BF16), pltpu.VMEM((width, width), BF16), dma((4,))],
        cost_estimate=cost(6, 9),
        compiler_params=params(24),
        name="prepare_roots",
    )(table, left_root, right_root, other_core(left_root), other_core(right_root))
    mine = pl.pallas_call(
        extract_kernel,
        out_shape=jax.ShapeDtypeStruct((width, width // 2), BF16),
        in_specs=[vmem, hbm],
        out_specs=vmem,
        scratch_shapes=[pltpu.VMEM((dp_count, groups, 8, LANES), F32)],
        cost_estimate=cost(0.6, 3),
        compiler_params=params(16),
        name="extract_extra",
    )(arrived, in_hbm(left1))
    other = other_core(mine)
    first = pl.pallas_call(
        first_kernel,
        out_shape=HBM(message_shape, BF16),
        in_specs=[vmem, vmem, vmem],
        out_specs=hbm,
        scratch_shapes=[
            pltpu.VMEM((width, wide), BF16),
            pltpu.VMEM((dp_count, mp_count, row_part, LANES), BF16),
            dma((len(FIRST_SPANS),)),
        ],
        cost_estimate=cost(4, 9),
        compiler_params=params(20),
        name="precondition_first",
    )(arrived, left0, padded)
    leaving, halves = pl.pallas_call(
        extra_kernel,
        out_shape=[HBM(message_shape, BF16), HBM((width, width), BF16)],
        in_specs=[vmem] * 4 + [hbm],
        out_specs=[hbm, hbm],
        input_output_aliases={4: 0},
        scratch_shapes=[
            pltpu.VMEM(message_shape, BF16),
            pltpu.VMEM((width, width), BF16),
            pltpu.VMEM((max(SPANS) * row_part, wide), BF16),
            dma((len(SPANS),)),
            dma((len(SPANS),)),
            dma,
        ],
        cost_estimate=cost(3, 9),
        compiler_params=params(20),
        name="precondition_extra",
    )(mine, other, left1, picked, first)
    returned = exchange(leaving.reshape(outgoing.shape))
    tile = width // 3
    stat_spec = pl.BlockSpec((1, tile, width), lambda s, i: (s, i, 0))
    left_new, right_new = pl.pallas_call(
        pair_gram_kernel,
        grid=(slots, width // tile),
        out_shape=[jax.ShapeDtypeStruct((slots, width, width), F32)] * 2,
        in_specs=[
            smem,
            pl.BlockSpec(message_shape, lambda s, i: (0, 0, 0, 0)),
            pl.BlockSpec((width, width), lambda s, i: (0, 0)),
            stat_spec,
            stat_spec,
        ],
        out_specs=[stat_spec, stat_spec],
        scratch_shapes=[pltpu.VMEM((width, wide), BF16), pltpu.VMEM((width, width), BF16)],
        cost_estimate=cost(9, 25),
        compiler_params=params(24),
        name="pair_grams",
    )(table, in_hbm(arrived), halves, left_stat[0, 0], right_stat[0, 0])
    precond = pl.pallas_call(
        unpack_pairs_kernel,
        out_shape=HBM(gradient.shape, BF16),
        in_specs=[hbm, hbm, vmem],
        out_specs=hbm,
        scratch_shapes=[
            pltpu.SMEM(owner.shape, jnp.int32),
            pltpu.SMEM(table.shape, jnp.int32),
            pltpu.VMEM(gradient.shape, BF16),
            pltpu.VMEM((2, row_part * col_blocks, LANES), F32),
            dma((2,)),
            dma((pieces,)),
        ],
        compiler_params=params(12),
        name="unpack_pairs",
    )(in_hbm(owner), in_hbm(table), returned)
    return (precond, left_new[None, None], right_new[None, None])


def per_device(gradient, owner, left_stat, right_stat, left_root, right_root):
    row_blocks, row_part, col_blocks, col_part = gradient.shape
    devices = lax.axis_size("dp") * lax.axis_size("mp")
    height = row_part + 8
    hbm = pl.BlockSpec(memory_space=HBM)
    dma = pltpu.SemaphoreType.DMA
    outgoing, table, bad = pl.pallas_call(
        pack_pairs_kernel,
        out_shape=[
            HBM((devices, height, LANES), BF16),
            HBM((2 * devices + LANES,), jnp.int32),
            HBM((LANES,), jnp.int32),
        ],
        in_specs=[hbm, hbm],
        out_specs=[hbm, hbm, hbm],
        scratch_shapes=[
            pltpu.SMEM(owner.shape, jnp.int32),
            pltpu.VMEM(gradient.shape, BF16),
            pltpu.VMEM((devices, height, LANES), BF16),
            pltpu.VMEM(((row_blocks + 1) * row_part * col_blocks, LANES), F32),
            pltpu.SMEM((2 * devices + LANES,), jnp.int32),
            pltpu.SMEM((LANES,), jnp.int32),
            pltpu.SMEM((devices,), jnp.int32),
            pltpu.SMEM((devices + 1,), jnp.int32),
            pltpu.SMEM((devices,), jnp.int32),
            dma((4,)),
            dma((4,)),
            dma((3,)),
        ],
        compiler_params=pltpu.CompilerParams(vmem_limit_bytes=16 * MIB),
        name="pack_pairs",
    )(owner, gradient)
    rest = (gradient, owner, left_stat, right_stat, left_root, right_root)
    if not FALLBACK:
        return pair_path(outgoing, table, *rest)
    return lax.cond(bad[0] == 0, pair_path, lambda outgoing, table, *rest: general_path(*rest), outgoing, table, *rest)


def solution(mesh):
    return jax.shard_map(
        per_device,
        mesh=mesh,
        in_specs=(
            P(None, "dp", None, "mp"),
            P(),
            P("dp", "mp", None, None, None),
            P("dp", "mp", None, None, None),
            P("dp", "mp", None, None, None),
            P("dp", "mp", None, None, None),
        ),
        out_specs=(
            P(None, "dp", None, "mp"),
            P("dp", "mp", None, None, None),
            P("dp", "mp", None, None, None),
        ),
        check_vma=False,
    )
```

```python
import jax
import jax.numpy as jnp
from jax import lax
from jax.experimental import pallas as pl
from jax.experimental.pallas import tpu as pltpu
from jax.sharding import PartitionSpec as P

STAT_DECAY = 0.98
LANES = 128
F32 = jnp.float32
BF16 = jnp.bfloat16
MIB = 1024 * 1024
FALLBACK = True
HBM = pltpu.HBM
SPANS = (8, 4, 4)


def spread_matrix(part, groups):
    row = lax.broadcasted_iota(jnp.int32, (groups * LANES, groups * part), 0)
    col = lax.broadcasted_iota(jnp.int32, (groups * LANES, groups * part), 1)
    hit = (row // LANES == col // part) & (row % LANES == col % part)
    return jnp.where(hit, 1.0, 0.0).astype(BF16)


def count_slots(owner_ref, seen_ref, block):
    dest = owner_ref[block]
    slot = seen_ref[dest]
    seen_ref[dest] = slot + 1
    return dest, slot


def clear_counts(seen_ref, devices):
    def clear(i, carry):
        seen_ref[i] = 0
        return carry

    lax.fori_loop(0, devices, clear, 0)


def pack_kernel(owner_ref, grad_ref, out_ref, rows_ref, seen_ref):
    row_blocks, row_part, col_blocks, col_part = grad_ref.shape
    devices, slots = out_ref.shape[:2]
    clear_counts(seen_ref, devices)
    rows_ref[...] = jnp.zeros_like(rows_ref)

    def clear(i, carry):
        for s in range(slots):
            out_ref[i, s] = jnp.zeros((row_part, LANES), BF16)
        return carry

    lax.fori_loop(0, devices, clear, 0)

    def block_row(r, carry):
        rows_ref[:, :col_part] = grad_ref[r].astype(F32).reshape(row_part * col_blocks, col_part)
        for c in range(col_blocks):
            dest, slot = count_slots(owner_ref, seen_ref, r * col_blocks + c)
            tile = rows_ref[pl.ds(c, row_part, stride=col_blocks), :]
            out_ref[dest, slot] = tile.astype(BF16)
        return carry

    lax.fori_loop(0, row_blocks, block_row, 0)


def unpack_kernel(owner_ref, back_ref, out_ref, rows_ref, seen_ref):
    row_blocks, row_part, col_blocks, col_part = out_ref.shape
    devices = back_ref.shape[0]
    clear_counts(seen_ref, devices)

    def block_row(r, carry):
        for c in range(col_blocks):
            dest, slot = count_slots(owner_ref, seen_ref, r * col_blocks + c)
            rows_ref[pl.ds(c, row_part, stride=col_blocks), :] = back_ref[dest, slot].astype(F32)
        rows = rows_ref[:, :col_part].reshape(row_part, col_blocks, col_part)
        out_ref[r] = rows.astype(BF16)
        return carry

    lax.fori_loop(0, row_blocks, block_row, 0)


def pad_kernel(root_ref, out_ref):
    width = root_ref.shape[1]
    part = width // (out_ref.shape[1] // LANES)
    groups = LANES // (LANES - part)
    spread = spread_matrix(part, groups)
    wide, narrow = spread.shape
    for g in range(width // narrow):
        rows = jnp.dot(spread, root_ref[0, g * narrow : (g + 1) * narrow, :], preferred_element_type=F32).astype(BF16)
        for h in range(width // narrow):
            cell = lax.dot_general(
                rows[:, h * narrow : (h + 1) * narrow], spread, (((1,), (1,)), ((), ())), preferred_element_type=F32
            )
            out_ref[0, g * wide : (g + 1) * wide, h * wide : (h + 1) * wide] = cell.astype(BF16)


def gather_tiles(arr_ref, wide_ref):
    row_groups, col_groups, _, row_part, _ = arr_ref.shape
    for a in range(row_groups):
        for m in range(col_groups):
            wide_ref[a * row_part : (a + 1) * row_part, m * LANES : (m + 1) * LANES] = arr_ref[a, m, 0]


def precond_kernel(arr_ref, left_ref, right_ref, out_ref, wide_ref):
    row_groups, col_groups, _, row_part, _ = arr_ref.shape
    gather_tiles(arr_ref, wide_ref)
    step = 4 * row_part
    for i in range(row_groups // 4):
        half = jnp.dot(left_ref[0, i * step : (i + 1) * step, :], wide_ref[...], preferred_element_type=F32).astype(BF16)
        result = jnp.dot(half, right_ref[0], preferred_element_type=F32).astype(BF16)
        for k in range(4):
            for m in range(col_groups):
                out_ref[4 * i + k, m, 0] = result[k * row_part : (k + 1) * row_part, m * LANES : (m + 1) * LANES]


def gram_kernel(arr_ref, left_ref, right_ref, left_out, right_out, wide_ref, block_ref):
    width = block_ref.shape[0]
    part = width // arr_ref.shape[1]
    tile = left_ref.shape[1]
    step = pl.program_id(1)

    @pl.when(step == 0)
    def _():
        gather_tiles(arr_ref, wide_ref)
        spread = spread_matrix(part, LANES // (LANES - part))
        wide, narrow = spread.shape
        for g in range(width // narrow):
            cols = jnp.dot(wide_ref[:, g * wide : (g + 1) * wide], spread, preferred_element_type=F32)
            block_ref[:, g * narrow : (g + 1) * narrow] = cols.astype(BF16)

    for i in range(width // tile):

        @pl.when(step == i)
        def _(i=i):
            mine = slice(i * tile, (i + 1) * tile)
            left = lax.dot_general(
                block_ref[mine, :], block_ref[...], (((1,), (1,)), ((), ())), preferred_element_type=F32
            )
            left_out[0] = STAT_DECAY * left_ref[0] + (1.0 - STAT_DECAY) * left
            right = lax.dot_general(
                block_ref[:, mine], block_ref[...], (((0,), (0,)), ((), ())), preferred_element_type=F32
            )
            right_out[0] = STAT_DECAY * right_ref[0] + (1.0 - STAT_DECAY) * right


def general_path(gradient, owner, left_stat, right_stat, left_root, right_root):
    row_blocks, row_part, col_blocks, col_part = gradient.shape
    dp_count = lax.axis_size("dp")
    mp_count = lax.axis_size("mp")
    devices = dp_count * mp_count
    slots, width = left_stat.shape[2:4]
    wide = mp_count * LANES
    smem = pl.BlockSpec(memory_space=pltpu.SMEM)
    vmem = pl.BlockSpec(memory_space=pltpu.VMEM)
    rows_scratch = pltpu.VMEM((row_part * col_blocks, LANES), F32)
    seen_scratch = pltpu.SMEM((devices,), jnp.int32)

    def exchange(x):
        return lax.all_to_all(x, ("dp", "mp"), split_axis=0, concat_axis=0, tiled=True)

    outgoing = pl.pallas_call(
        pack_kernel,
        out_shape=jax.ShapeDtypeStruct((devices, slots, row_part, LANES), BF16),
        in_specs=[smem, vmem],
        out_specs=vmem,
        scratch_shapes=[rows_scratch, seen_scratch],
        compiler_params=pltpu.CompilerParams(vmem_limit_bytes=12 * MIB),
        name="pack",
    )(owner, gradient)
    padded_root = pl.pallas_call(
        pad_kernel,
        grid=(slots,),
        out_shape=jax.ShapeDtypeStruct((slots, wide, wide), BF16),
        in_specs=[pl.BlockSpec((1, width, width), lambda s: (s, 0, 0))],
        out_specs=pl.BlockSpec((1, wide, wide), lambda s: (s, 0, 0)),
        cost_estimate=pl.CostEstimate(flops=slots * 4 * 10**9, bytes_accessed=7 * 10**6, transcendentals=0),
        compiler_params=pltpu.CompilerParams(vmem_limit_bytes=24 * MIB),
        name="pad_right_root",
    )(right_root[0, 0])
    tiles = (dp_count, mp_count, slots, row_part, LANES)
    arrived = exchange(outgoing).reshape(tiles)
    tile_spec = pl.BlockSpec((dp_count, mp_count, 1, row_part, LANES), lambda s, *_: (0, 0, s, 0, 0))
    leaving = pl.pallas_call(
        precond_kernel,
        grid=(slots,),
        out_shape=jax.ShapeDtypeStruct(tiles, BF16),
        in_specs=[
            tile_spec,
            pl.BlockSpec((1, width, width), lambda s: (s, 0, 0)),
            pl.BlockSpec((1, wide, wide), lambda s: (s, 0, 0)),
        ],
        out_specs=tile_spec,
        scratch_shapes=[pltpu.VMEM((width, wide), BF16)],
        cost_estimate=pl.CostEstimate(flops=slots * 3 * 10**9, bytes_accessed=13 * 10**6, transcendentals=0),
        compiler_params=pltpu.CompilerParams(vmem_limit_bytes=30 * MIB),
        name="precondition",
    )(arrived, left_root[0, 0], padded_root)
    returned = exchange(leaving.reshape(outgoing.shape))
    tile = width // 3
    stat_spec = pl.BlockSpec((1, tile, width), lambda s, i: (s, i, 0))
    left_new, right_new = pl.pallas_call(
        gram_kernel,
        grid=(slots, width // tile),
        out_shape=[jax.ShapeDtypeStruct((slots, width, width), F32)] * 2,
        in_specs=[tile_spec, stat_spec, stat_spec],
        out_specs=[stat_spec, stat_spec],
        scratch_shapes=[pltpu.VMEM((width, wide), BF16), pltpu.VMEM((width, width), BF16)],
        cost_estimate=pl.CostEstimate(flops=slots * 3 * 10**9, bytes_accessed=22 * 10**6, transcendentals=0),
        compiler_params=pltpu.CompilerParams(vmem_limit_bytes=30 * MIB),
        name="grams",
    )(arrived, left_stat[0, 0], right_stat[0, 0])
    precond = pl.pallas_call(
        unpack_kernel,
        out_shape=jax.ShapeDtypeStruct(gradient.shape, BF16),
        in_specs=[smem, vmem],
        out_specs=vmem,
        scratch_shapes=[rows_scratch, seen_scratch],
        compiler_params=pltpu.CompilerParams(vmem_limit_bytes=12 * MIB),
        name="unpack",
    )(owner, returned)
    return (precond, left_new[None, None], right_new[None, None])


def copy_in(src, dst, sem):
    copy = pltpu.make_async_copy(src, dst, sem)
    copy.start()
    return copy


def lane_of(shape):
    return lax.broadcasted_iota(jnp.int32, shape, len(shape) - 1)


def pack_pairs_kernel(
    owner_hbm, grad_hbm, out_hbm, table_hbm, bad_hbm, owner_ref, grad_ref, out_ref, rows_ref, table_ref, bad_ref, seen_ref, first_ref,
    pairs_ref, load_sems, store_sems, sems,
):
    row_blocks, row_part, col_blocks, col_part = grad_ref.shape
    devices, height = out_hbm.shape[:2]
    count = row_blocks * col_blocks
    tall = row_part * col_blocks
    chunks = load_sems.shape[0]
    span = row_blocks // chunks
    owner_copy = copy_in(owner_hbm, owner_ref, sems.at[0])
    copies = []
    for i in range(chunks):
        part = pl.ds(i * span, span)
        copies.append(copy_in(grad_hbm.at[part], grad_ref.at[part], load_sems.at[i]))
    me = lax.axis_index("dp") * lax.axis_size("mp") + lax.axis_index("mp")
    half = col_part // 2
    free = LANES - col_part
    rest = half - free
    groups = row_part // 8
    extras_at = devices
    info_at = 2 * devices

    def clear(i, carry):
        seen_ref[i] = 0
        pairs_ref[i] = 0
        first_ref[i] = count
        return carry

    lax.fori_loop(0, devices, clear, 0, unroll=8)
    rows_ref[pl.ds(row_blocks * tall, tall), :] = jnp.zeros((tall, LANES), F32)
    owner_copy.wait()

    def block_row(r, extras):
        rows_ref[pl.ds(r * tall, tall), col_part:] = jnp.zeros((tall, free), F32)
        rows_ref[pl.ds(r * tall, tall), :col_part] = grad_ref[r].astype(F32).reshape(tall, col_part)
        for c in range(col_blocks):
            block = r * col_blocks + c
            dest, slot = count_slots(owner_ref, seen_ref, block)
            table_ref[block] = jnp.where(slot == 0, dest, 0)
            first_ref[jnp.where(slot == 0, dest, devices)] = block
            table_ref[extras_at + extras] = block
            extras = extras + slot
        return extras

    extras = jnp.int32(0)
    for i in range(chunks):
        copies[i].wait()
        extras = lax.fori_loop(i * span, (i + 1) * span, block_row, extras)
    for i in range(3):
        table_ref[info_at + i] = 0
    table_ref[info_at + 3] = extras
    bad_ref[0] = 0

    def note(e, carry):
        dest = owner_ref[table_ref[extras_at + e]]
        pairs = pairs_ref[dest // 2]
        pairs_ref[dest // 2] = pairs + 1
        here = dest // 2 == me // 2
        table_ref[info_at] = jnp.where(here, 1, table_ref[info_at])
        table_ref[info_at + 1] = jnp.where(here, dest % 2, table_ref[info_at + 1])
        table_ref[info_at + 2] = jnp.where(dest == me, 1, table_ref[info_at + 2])
        bad_ref[0] = jnp.where(pairs > 0, 1, bad_ref[0])
        return carry

    lax.fori_loop(0, extras, note, 0)
    table_copy = copy_in(table_ref, table_hbm, sems.at[1])
    bad_copy = copy_in(bad_ref, bad_hbm, sems.at[2])

    def tile_of(block):
        return rows_ref[pl.ds(block // col_blocks * tall + block % col_blocks, row_part, stride=col_blocks), :]

    def message(d, carry):
        tile = tile_of(first_ref[d])
        out_ref[d] = jnp.concatenate([tile, jnp.zeros((height - row_part, LANES), F32)], axis=0).astype(BF16)
        return carry

    stores = []
    pieces = store_sems.shape[0]
    share = devices // pieces
    for i in range(pieces):
        lax.fori_loop(i * share, (i + 1) * share, message, 0, unroll=8)

        def extra(e, carry, i=i):
            block = table_ref[extras_at + e]
            chip = owner_ref[block] // 2

            @pl.when(2 * chip // share == i)
            def _():
                tile = tile_of(block)
                lane = lane_of((row_part, LANES))
                lane8 = lane_of((8, LANES))
                for j in range(2):
                    old = out_ref[2 * chip + j].astype(F32)
                    moved = pltpu.roll(tile, (col_part - half * j) % LANES, 1)
                    top = jnp.where(lane < col_part, old[:row_part], moved)
                    low = jnp.zeros((8, LANES), F32)
                    for k in range(groups):
                        piece = pltpu.roll(tile[8 * k : 8 * k + 8], (rest * k - half * j - free) % LANES, 1)
                        low = jnp.where(lane8 // rest == k, piece, low)
                    out_ref[2 * chip + j] = jnp.concatenate([top, low], axis=0).astype(BF16)

            return carry

        lax.fori_loop(0, extras, extra, 0)
        part = pl.ds(i * share, share)
        stores.append(copy_in(out_ref.at[part], out_hbm.at[part], store_sems.at[i]))
    table_copy.wait()
    bad_copy.wait()
    for store in stores:
        store.wait()


def unpack_pairs_kernel(owner_hbm, table_hbm, back_ref, out_hbm, owner_ref, table_ref, out_ref, rows_ref, sems, store_sems):
    row_blocks, row_part, col_blocks, col_part = out_ref.shape
    devices = back_ref.shape[0]
    owner_copy = copy_in(owner_hbm, owner_ref, sems.at[0])
    table_copy = copy_in(table_hbm, table_ref, sems.at[1])
    half = col_part // 2
    free = LANES - col_part
    rest = half - free
    groups = row_part // 8
    chunks = store_sems.shape[0]
    span = row_blocks // chunks
    owner_copy.wait()
    table_copy.wait()

    def finish(r, buffer):
        rows = rows_ref[buffer, :, :col_part].reshape(row_part, col_blocks, col_part)
        out_ref[r] = rows.astype(BF16)

    def block_row(r, buffer):
        for c in range(col_blocks):
            tile = back_ref[table_ref[r * col_blocks + c], :row_part, :]
            rows_ref[buffer, pl.ds(c, row_part, stride=col_blocks), :] = tile.astype(F32)
        finish(r, buffer)

    def body(t, carry):
        block_row(2 * t, 0)
        block_row(2 * t + 1, 1)
        return carry

    stores = []
    for i in range(chunks):
        lax.fori_loop(i * span // 2, (i + 1) * span // 2, body, 0)

        def extra(e, carry, i=i):
            block = table_ref[devices + e]
            chip = owner_ref[block] // 2
            r = block // col_blocks

            @pl.when(r // span == i)
            def _():
                lane = lane_of((row_part, LANES))
                tile = jnp.zeros((row_part, LANES), F32)
                for j in range(2):
                    message = back_ref[2 * chip + j].astype(F32)
                    top = pltpu.roll(message[:row_part], (half * j - col_part) % LANES, 1)
                    low = [
                        pltpu.roll(message[row_part : row_part + 8], (half * j + free - rest * k) % LANES, 1)
                        for k in range(groups)
                    ]
                    low = jnp.concatenate(low, axis=0)
                    tile = jnp.where((lane >= half * j) & (lane < half * j + free), top, tile)
                    tile = jnp.where((lane >= half * j + free) & (lane < half * j + half), low, tile)
                rows_ref[0, :, :col_part] = out_ref[r].astype(F32).reshape(row_part * col_blocks, col_part)
                rows_ref[0, pl.ds(block % col_blocks, row_part, stride=col_blocks), :] = tile
                finish(r, 0)

            return carry

        lax.fori_loop(0, table_ref[2 * devices + 3], extra, 0)
        part = pl.ds(i * span, span)
        stores.append(copy_in(out_ref.at[part], out_hbm.at[part], store_sems.at[i]))
    for store in stores:
        store.wait()


def halves_order(shape, core, axis, part, groups):
    half = part // 2
    free = LANES - part
    rest = half - free
    n = lax.broadcasted_iota(jnp.int32, shape, axis)
    tail = n - free * groups
    first = part * (n // free) + n % free
    second = part * (tail // rest) + free + tail % rest
    return half * core + jnp.where(tail < 0, first, second)


def swap_groups(rows, rest):
    rows = list(rows)
    count = len(rows)
    group = lane_of(rows[0].shape) // rest
    bit = 1
    while bit < count:
        low = group // bit % 2 == 0
        for i in range(count):
            if i // bit % 2 == 0:
                x, y = rows[i], rows[i + bit]
                rows[i] = jnp.where(low, x, pltpu.roll(y, rest * bit, 1))
                rows[i + bit] = jnp.where(low, pltpu.roll(x, LANES - rest * bit, 1), y)
        bit *= 2
    return rows


def prepare_kernel(
    table_ref, left_hbm, right_hbm, left_other_hbm, right_other_hbm, padded_ref, picked_ref, left0_ref, left1_ref, root_ref, root1_ref,
    sems,
):
    width = root_ref.shape[0]
    groups = padded_ref.shape[0] // LANES
    part = width // groups
    half = width // 2
    core = lax.axis_index("mp") % 2
    info_at = table_ref.shape[0] - LANES
    left0_copy = copy_in(left_hbm.at[0], left0_ref, sems.at[0])
    root_copy = copy_in(right_hbm.at[0], root_ref, sems.at[1])
    from_other = (table_ref[info_at] == 1) & (table_ref[info_at + 1] != core)

    @pl.when(from_other)
    def _():
        right = copy_in(right_other_hbm.at[1], root1_ref, sems.at[2])
        copy_in(left_other_hbm.at[1], left1_ref, sems.at[3]).wait()
        right.wait()

    @pl.when(jnp.logical_not(from_other))
    def _():
        right = copy_in(right_hbm.at[1], root1_ref, sems.at[2])
        copy_in(left_hbm.at[1], left1_ref, sems.at[3]).wait()
        right.wait()

    mine = jnp.where(
        halves_order((width, half), core, 1, part, groups) == lax.broadcasted_iota(jnp.int32, (width, half), 0), 1.0, 0.0
    ).astype(BF16)
    cols = jnp.dot(root1_ref[...], mine, preferred_element_type=F32).astype(BF16)
    for j in range(2):
        theirs = jnp.where(
            halves_order((half, width), j, 0, part, groups) == lax.broadcasted_iota(jnp.int32, (half, width), 1), 1.0, 0.0
        ).astype(BF16)
        picked_ref[j * half : (j + 1) * half, :] = jnp.dot(theirs, cols, preferred_element_type=F32).astype(BF16)
    root_copy.wait()
    spread = spread_matrix(part, LANES // (LANES - part))
    wide, narrow = spread.shape
    for g in range(width // narrow):
        rows = jnp.dot(spread, root_ref[g * narrow : (g + 1) * narrow, :], preferred_element_type=F32).astype(BF16)
        for h in range(width // narrow):
            cell = lax.dot_general(
                rows[:, h * narrow : (h + 1) * narrow], spread, (((1,), (1,)), ((), ())), preferred_element_type=F32
            )
            padded_ref[g * wide : (g + 1) * wide, h * wide : (h + 1) * wide] = cell.astype(BF16)
    left0_copy.wait()


def take_matrix(part):
    free = LANES - part
    shape = ((LANES // free) * LANES, LANES)
    row = lax.broadcasted_iota(jnp.int32, shape, 0)
    col = lax.broadcasted_iota(jnp.int32, shape, 1)
    return jnp.where((row // LANES == col // free) & (row % LANES == part + col % free), 1.0, 0.0).astype(BF16)


def extract_kernel(arr_ref, roots_hbm, out_ref, tall_ref):
    row_groups, col_groups, height, _ = arr_ref.shape
    row_part = height - 8
    width = row_groups * row_part
    part = width // col_groups
    take = take_matrix(part)
    span = take.shape[0] // LANES
    for g in range(col_groups // span):
        tiles = [arr_ref[:, g * span + m, :row_part, :].reshape(width, LANES) for m in range(span)]
        cols = jnp.dot(jnp.concatenate(tiles, axis=1), take, preferred_element_type=F32)
        out_ref[:, g * LANES : (g + 1) * LANES] = cols.astype(BF16)
    low = [arr_ref[:, m, row_part:, :].astype(F32).reshape(8 * row_groups, LANES) for m in range(col_groups)]
    low = swap_groups(low, LANES // col_groups)
    for k in range(row_part // 8):
        tall_ref[:, k] = low[k].reshape(row_groups, 8, LANES)
    out_ref[:, width // 2 - LANES :] = tall_ref[...].reshape(width, LANES).astype(BF16)


def half_kernel(arr_ref, left_ref, half_ref, wide_hbm, wide_ref, sem):
    row_groups, col_groups, height, _ = arr_ref.shape
    row_part = height - 8
    for a in range(row_groups):
        for m in range(col_groups):
            wide_ref[a * row_part : (a + 1) * row_part, m * LANES : (m + 1) * LANES] = arr_ref[a, m, :row_part, :]
    wide_copy = copy_in(wide_ref, wide_hbm, sem)
    step = left_ref.shape[0] // 2
    for i in range(2):
        rows = slice(i * step, (i + 1) * step)
        half_ref[rows, :] = jnp.dot(left_ref[rows, :], wide_ref[...], preferred_element_type=F32).astype(BF16)
    wide_copy.wait()


def products_kernel(
    half_ref, right0_ref, mine_ref, other_ref, left1_hbm, right1_hbm, out_hbm, block_hbm, block_ref, left1_ref, right1_ref, top_ref,
    message_ref, store_sems, sems,
):
    row_groups, col_groups, height, _ = message_ref.shape
    row_part = height - 8
    width = left1_ref.shape[0]
    half = width // 2
    groups = row_part // 8
    core = lax.axis_index("mp") % 2
    left1_copy = copy_in(left1_hbm, left1_ref, sems.at[0])
    right1_copy = copy_in(right1_hbm, right1_ref, sems.at[1])
    for j in range(2):

        @pl.when(core == j)
        def _(j=j):
            block_ref[:, j * half : (j + 1) * half] = mine_ref[...]
            block_ref[:, (1 - j) * half : (2 - j) * half] = other_ref[...]

    block_copy = copy_in(block_ref, block_hbm, sems.at[2])
    take = take_matrix(width // col_groups)
    wide = take.shape[0]
    transposed = (((1,), (1,)), ((), ()))
    stores = []
    start = 0
    for i, span in enumerate(SPANS):
        rows = slice(start * row_part, (start + span) * row_part)
        first = jnp.dot(half_ref[rows, :], right0_ref[...], preferred_element_type=F32).astype(BF16)
        for k in range(span):
            for m in range(col_groups):
                message_ref[start + k, m, :row_part] = first[k * row_part : (k + 1) * row_part, m * LANES : (m + 1) * LANES]
        if i == 0:
            left1_copy.wait()
            right1_copy.wait()
        temp = jnp.dot(left1_ref[rows, :], block_ref[...], preferred_element_type=F32).astype(BF16)
        extra = jnp.dot(temp, right1_ref[...], preferred_element_type=F32)
        top = extra[:, : half - LANES].astype(BF16)
        for g in range(col_groups * LANES // wide):
            spread = lax.dot_general(top[:, g * LANES : (g + 1) * LANES], take, transposed, preferred_element_type=F32)
            top_ref[: span * row_part, g * wide : (g + 1) * wide] = spread.astype(BF16)
        low = extra[:, half - LANES :].reshape(span, groups, 8, LANES)
        low = [low[:, k].reshape(8 * span, LANES) for k in range(groups)]
        low += [jnp.zeros((8 * span, LANES), F32)] * (col_groups - groups)
        low = swap_groups(low, LANES // col_groups)
        for k in range(span):
            for m in range(col_groups):
                cols = slice(m * LANES, (m + 1) * LANES)
                message_ref[start + k, m, :row_part] += top_ref[k * row_part : (k + 1) * row_part, cols]
                message_ref[start + k, m, row_part:] = low[m][8 * k : 8 * k + 8].astype(BF16)
        part = pl.ds(start, span)
        stores.append(copy_in(message_ref.at[part], out_hbm.at[part], store_sems.at[i]))
        start += span
    block_copy.wait()
    for store in stores:
        store.wait()


def pair_gram_kernel(table_ref, wide_ref, halves_ref, left_ref, right_ref, left_out, right_out, block_ref):
    width = block_ref.shape[0]
    col_groups = wide_ref.shape[1] // LANES
    part = width // col_groups
    tile = left_ref.shape[1]
    slot = pl.program_id(0)
    step = pl.program_id(1)
    has_extra = table_ref[table_ref.shape[0] - LANES + 2]

    @pl.when((step == 0) & (slot == 0))
    def _():
        spread = spread_matrix(part, LANES // (LANES - part))
        wide, narrow = spread.shape
        for g in range(width // narrow):
            cols = jnp.dot(wide_ref[:, g * wide : (g + 1) * wide], spread, preferred_element_type=F32)
            block_ref[:, g * narrow : (g + 1) * narrow] = cols.astype(BF16)

    @pl.when((step == 0) & (slot == 1) & (has_extra == 1))
    def _():
        half = width // 2
        total = jnp.zeros((width, width), F32)
        for j in range(2):
            order = halves_order((half, width), j, 0, part, col_groups)
            theirs = jnp.where(order == lax.broadcasted_iota(jnp.int32, (half, width), 1), 1.0, 0.0).astype(BF16)
            total += jnp.dot(halves_ref[:, j * half : (j + 1) * half], theirs, preferred_element_type=F32)
        block_ref[...] = total.astype(BF16)

    @pl.when((step == 0) & (slot == 1) & (has_extra == 0))
    def _():
        block_ref[...] = jnp.zeros_like(block_ref)

    for i in range(width // tile):

        @pl.when(step == i)
        def _(i=i):
            mine = slice(i * tile, (i + 1) * tile)
            left = lax.dot_general(
                block_ref[mine, :], block_ref[...], (((1,), (1,)), ((), ())), preferred_element_type=F32
            )
            left_out[0] = STAT_DECAY * left_ref[0] + (1.0 - STAT_DECAY) * left
            right = lax.dot_general(
                block_ref[:, mine], block_ref[...], (((0,), (0,)), ((), ())), preferred_element_type=F32
            )
            right_out[0] = STAT_DECAY * right_ref[0] + (1.0 - STAT_DECAY) * right


def exchange(x):
    return lax.all_to_all(x, ("dp", "mp"), split_axis=0, concat_axis=0, tiled=True)


def other_core(x):
    count = lax.axis_size("mp")
    return lax.ppermute(x, "mp", [(i, i ^ 1) for i in range(count)])


def pair_path(outgoing, table, gradient, owner, left_stat, right_stat, left_root, right_root):
    row_blocks, row_part, col_blocks, col_part = gradient.shape
    dp_count = lax.axis_size("dp")
    mp_count = lax.axis_size("mp")
    devices = dp_count * mp_count
    slots, width = left_stat.shape[2:4]
    wide = mp_count * LANES
    height = outgoing.shape[1]
    groups = row_part // 8
    pieces = 4
    smem = pl.BlockSpec(memory_space=pltpu.SMEM)
    vmem = pl.BlockSpec(memory_space=pltpu.VMEM)
    hbm = pl.BlockSpec(memory_space=HBM)
    dma = pltpu.SemaphoreType.DMA
    message_shape = (dp_count, mp_count, height, LANES)
    left_root = left_root[0, 0]
    right_root = right_root[0, 0]

    def params(mib):
        return pltpu.CompilerParams(vmem_limit_bytes=mib * MIB)

    def cost(flops, moved):
        return pl.CostEstimate(flops=int(flops * 1e9), bytes_accessed=int(moved * 1e6), transcendentals=0)

    def in_hbm(x):
        return pltpu.with_memory_space_constraint(x, HBM)

    arrived = exchange(outgoing).reshape(message_shape)
    padded, picked, left0, left1 = pl.pallas_call(
        prepare_kernel,
        out_shape=[
            HBM((wide, wide), BF16),
            HBM((width, width // 2), BF16),
            HBM((width, width), BF16),
            HBM((width, width), BF16),
        ],
        in_specs=[smem, hbm, hbm, hbm, hbm],
        out_specs=[vmem] * 4,
        scratch_shapes=[pltpu.VMEM((width, width), BF16), pltpu.VMEM((width, width), BF16), dma((4,))],
        cost_estimate=cost(6, 9),
        compiler_params=params(24),
        name="prepare_roots",
    )(table, left_root, right_root, other_core(left_root), other_core(right_root))
    mine = pl.pallas_call(
        extract_kernel,
        out_shape=jax.ShapeDtypeStruct((width, width // 2), BF16),
        in_specs=[vmem, hbm],
        out_specs=vmem,
        scratch_shapes=[pltpu.VMEM((dp_count, groups, 8, LANES), F32)],
        cost_estimate=cost(0.6, 3),
        compiler_params=params(16),
        name="extract_extra",
    )(arrived, in_hbm(left1))
    other = other_core(mine)
    half, block = pl.pallas_call(
        half_kernel,
        out_shape=[pltpu.VMEM((width, wide), BF16), HBM((width, wide), BF16)],
        in_specs=[vmem, vmem],
        out_specs=[vmem, hbm],
        scratch_shapes=[pltpu.VMEM((width, wide), BF16), dma],
        cost_estimate=cost(2, 6),
        compiler_params=params(16),
        name="half_product",
    )(arrived, left0)
    leaving, halves = pl.pallas_call(
        products_kernel,
        out_shape=[HBM(message_shape, BF16), HBM((width, width), BF16)],
        in_specs=[vmem] * 4 + [hbm] * 2,
        out_specs=[hbm] * 2,
        scratch_shapes=[
            pltpu.VMEM((width, width), BF16),
            pltpu.VMEM((width, width), BF16),
            pltpu.VMEM((width, width // 2), BF16),
            pltpu.VMEM((max(SPANS) * row_part, wide), BF16),
            pltpu.VMEM(message_shape, BF16),
            dma((len(SPANS),)),
            dma((3,)),
        ],
        cost_estimate=cost(5, 12),
        compiler_params=params(28),
        name="precondition",
    )(half, padded, mine, other, in_hbm(left1), in_hbm(picked))
    returned = exchange(leaving.reshape(outgoing.shape))
    tile = width // 3
    stat_spec = pl.BlockSpec((1, tile, width), lambda s, i: (s, i, 0))
    left_new, right_new = pl.pallas_call(
        pair_gram_kernel,
        grid=(slots, width // tile),
        out_shape=[jax.ShapeDtypeStruct((slots, width, width), F32)] * 2,
        in_specs=[
            smem,
            pl.BlockSpec((width, wide), lambda s, i: (0, 0)),
            pl.BlockSpec((width, width), lambda s, i: (0, 0)),
            stat_spec,
            stat_spec,
        ],
        out_specs=[stat_spec, stat_spec],
        scratch_shapes=[pltpu.VMEM((width, width), BF16)],
        cost_estimate=cost(9, 25),
        compiler_params=params(24),
        name="pair_grams",
    )(table, in_hbm(block), in_hbm(halves), left_stat[0, 0], right_stat[0, 0])
    precond = pl.pallas_call(
        unpack_pairs_kernel,
        out_shape=HBM(gradient.shape, BF16),
        in_specs=[hbm, hbm, vmem],
        out_specs=hbm,
        scratch_shapes=[
            pltpu.SMEM(owner.shape, jnp.int32),
            pltpu.SMEM(table.shape, jnp.int32),
            pltpu.VMEM(gradient.shape, BF16),
            pltpu.VMEM((2, row_part * col_blocks, LANES), F32),
            dma((2,)),
            dma((pieces,)),
        ],
        compiler_params=params(12),
        name="unpack_pairs",
    )(in_hbm(owner), in_hbm(table), returned)
    return (precond, left_new[None, None], right_new[None, None])


def per_device(gradient, owner, left_stat, right_stat, left_root, right_root):
    row_blocks, row_part, col_blocks, col_part = gradient.shape
    devices = lax.axis_size("dp") * lax.axis_size("mp")
    height = row_part + 8
    hbm = pl.BlockSpec(memory_space=HBM)
    dma = pltpu.SemaphoreType.DMA
    outgoing, table, bad = pl.pallas_call(
        pack_pairs_kernel,
        out_shape=[
            HBM((devices, height, LANES), BF16),
            HBM((2 * devices + LANES,), jnp.int32),
            HBM((LANES,), jnp.int32),
        ],
        in_specs=[hbm, hbm],
        out_specs=[hbm, hbm, hbm],
        scratch_shapes=[
            pltpu.SMEM(owner.shape, jnp.int32),
            pltpu.VMEM(gradient.shape, BF16),
            pltpu.VMEM((devices, height, LANES), BF16),
            pltpu.VMEM(((row_blocks + 1) * row_part * col_blocks, LANES), F32),
            pltpu.SMEM((2 * devices + LANES,), jnp.int32),
            pltpu.SMEM((LANES,), jnp.int32),
            pltpu.SMEM((devices,), jnp.int32),
            pltpu.SMEM((devices + 1,), jnp.int32),
            pltpu.SMEM((devices,), jnp.int32),
            dma((2,)),
            dma((4,)),
            dma((3,)),
        ],
        compiler_params=pltpu.CompilerParams(vmem_limit_bytes=16 * MIB),
        name="pack_pairs",
    )(owner, gradient)
    rest = (gradient, owner, left_stat, right_stat, left_root, right_root)
    if not FALLBACK:
        return pair_path(outgoing, table, *rest)
    return lax.cond(bad[0] == 0, pair_path, lambda outgoing, table, *rest: general_path(*rest), outgoing, table, *rest)


def solution(mesh):
    return jax.shard_map(
        per_device,
        mesh=mesh,
        in_specs=(
            P(None, "dp", None, "mp"),
            P(),
            P("dp", "mp", None, None, None),
            P("dp", "mp", None, None, None),
            P("dp", "mp", None, None, None),
            P("dp", "mp", None, None, None),
        ),
        out_specs=(
            P(None, "dp", None, "mp"),
            P("dp", "mp", None, None, None),
            P("dp", "mp", None, None, None),
        ),
        check_vma=False,
    )
```

```python
import jax
import jax.numpy as jnp
from jax import lax
from jax.experimental import pallas as pl
from jax.experimental.pallas import tpu as pltpu
from jax.sharding import PartitionSpec as P

STAT_DECAY = 0.98
LANES = 128
F32 = jnp.float32
BF16 = jnp.bfloat16
MIB = 1024 * 1024
FALLBACK = True
HBM = pltpu.HBM
SPANS = (8, 4, 4)


def spread_matrix(part, groups):
    row = lax.broadcasted_iota(jnp.int32, (groups * LANES, groups * part), 0)
    col = lax.broadcasted_iota(jnp.int32, (groups * LANES, groups * part), 1)
    hit = (row // LANES == col // part) & (row % LANES == col % part)
    return jnp.where(hit, 1.0, 0.0).astype(BF16)


def count_slots(owner_ref, seen_ref, block):
    dest = owner_ref[block]
    slot = seen_ref[dest]
    seen_ref[dest] = slot + 1
    return dest, slot


def clear_counts(seen_ref, devices):
    def clear(i, carry):
        seen_ref[i] = 0
        return carry

    lax.fori_loop(0, devices, clear, 0)


def pack_kernel(owner_ref, grad_ref, out_ref, rows_ref, seen_ref):
    row_blocks, row_part, col_blocks, col_part = grad_ref.shape
    devices, slots = out_ref.shape[:2]
    clear_counts(seen_ref, devices)
    rows_ref[...] = jnp.zeros_like(rows_ref)

    def clear(i, carry):
        for s in range(slots):
            out_ref[i, s] = jnp.zeros((row_part, LANES), BF16)
        return carry

    lax.fori_loop(0, devices, clear, 0)

    def block_row(r, carry):
        rows_ref[:, :col_part] = grad_ref[r].astype(F32).reshape(row_part * col_blocks, col_part)
        for c in range(col_blocks):
            dest, slot = count_slots(owner_ref, seen_ref, r * col_blocks + c)
            tile = rows_ref[pl.ds(c, row_part, stride=col_blocks), :]
            out_ref[dest, slot] = tile.astype(BF16)
        return carry

    lax.fori_loop(0, row_blocks, block_row, 0)


def unpack_kernel(owner_ref, back_ref, out_ref, rows_ref, seen_ref):
    row_blocks, row_part, col_blocks, col_part = out_ref.shape
    devices = back_ref.shape[0]
    clear_counts(seen_ref, devices)

    def block_row(r, carry):
        for c in range(col_blocks):
            dest, slot = count_slots(owner_ref, seen_ref, r * col_blocks + c)
            rows_ref[pl.ds(c, row_part, stride=col_blocks), :] = back_ref[dest, slot].astype(F32)
        rows = rows_ref[:, :col_part].reshape(row_part, col_blocks, col_part)
        out_ref[r] = rows.astype(BF16)
        return carry

    lax.fori_loop(0, row_blocks, block_row, 0)


def pad_kernel(root_ref, out_ref):
    width = root_ref.shape[1]
    part = width // (out_ref.shape[1] // LANES)
    groups = LANES // (LANES - part)
    spread = spread_matrix(part, groups)
    wide, narrow = spread.shape
    for g in range(width // narrow):
        rows = jnp.dot(spread, root_ref[0, g * narrow : (g + 1) * narrow, :], preferred_element_type=F32).astype(BF16)
        for h in range(width // narrow):
            cell = lax.dot_general(
                rows[:, h * narrow : (h + 1) * narrow], spread, (((1,), (1,)), ((), ())), preferred_element_type=F32
            )
            out_ref[0, g * wide : (g + 1) * wide, h * wide : (h + 1) * wide] = cell.astype(BF16)


def gather_tiles(arr_ref, wide_ref):
    row_groups, col_groups, _, row_part, _ = arr_ref.shape
    for a in range(row_groups):
        for m in range(col_groups):
            wide_ref[a * row_part : (a + 1) * row_part, m * LANES : (m + 1) * LANES] = arr_ref[a, m, 0]


def precond_kernel(arr_ref, left_ref, right_ref, out_ref, wide_ref):
    row_groups, col_groups, _, row_part, _ = arr_ref.shape
    gather_tiles(arr_ref, wide_ref)
    step = 4 * row_part
    for i in range(row_groups // 4):
        half = jnp.dot(left_ref[0, i * step : (i + 1) * step, :], wide_ref[...], preferred_element_type=F32).astype(BF16)
        result = jnp.dot(half, right_ref[0], preferred_element_type=F32).astype(BF16)
        for k in range(4):
            for m in range(col_groups):
                out_ref[4 * i + k, m, 0] = result[k * row_part : (k + 1) * row_part, m * LANES : (m + 1) * LANES]


def gram_kernel(arr_ref, left_ref, right_ref, left_out, right_out, wide_ref, block_ref):
    width = block_ref.shape[0]
    part = width // arr_ref.shape[1]
    tile = left_ref.shape[1]
    step = pl.program_id(1)

    @pl.when(step == 0)
    def _():
        gather_tiles(arr_ref, wide_ref)
        spread = spread_matrix(part, LANES // (LANES - part))
        wide, narrow = spread.shape
        for g in range(width // narrow):
            cols = jnp.dot(wide_ref[:, g * wide : (g + 1) * wide], spread, preferred_element_type=F32)
            block_ref[:, g * narrow : (g + 1) * narrow] = cols.astype(BF16)

    for i in range(width // tile):

        @pl.when(step == i)
        def _(i=i):
            mine = slice(i * tile, (i + 1) * tile)
            left = lax.dot_general(
                block_ref[mine, :], block_ref[...], (((1,), (1,)), ((), ())), preferred_element_type=F32
            )
            left_out[0] = STAT_DECAY * left_ref[0] + (1.0 - STAT_DECAY) * left
            right = lax.dot_general(
                block_ref[:, mine], block_ref[...], (((0,), (0,)), ((), ())), preferred_element_type=F32
            )
            right_out[0] = STAT_DECAY * right_ref[0] + (1.0 - STAT_DECAY) * right


def general_path(gradient, owner, left_stat, right_stat, left_root, right_root):
    row_blocks, row_part, col_blocks, col_part = gradient.shape
    dp_count = lax.axis_size("dp")
    mp_count = lax.axis_size("mp")
    devices = dp_count * mp_count
    slots, width = left_stat.shape[2:4]
    wide = mp_count * LANES
    smem = pl.BlockSpec(memory_space=pltpu.SMEM)
    vmem = pl.BlockSpec(memory_space=pltpu.VMEM)
    rows_scratch = pltpu.VMEM((row_part * col_blocks, LANES), F32)
    seen_scratch = pltpu.SMEM((devices,), jnp.int32)

    def exchange(x):
        return lax.all_to_all(x, ("dp", "mp"), split_axis=0, concat_axis=0, tiled=True)

    outgoing = pl.pallas_call(
        pack_kernel,
        out_shape=jax.ShapeDtypeStruct((devices, slots, row_part, LANES), BF16),
        in_specs=[smem, vmem],
        out_specs=vmem,
        scratch_shapes=[rows_scratch, seen_scratch],
        compiler_params=pltpu.CompilerParams(vmem_limit_bytes=12 * MIB),
        name="pack",
    )(owner, gradient)
    padded_root = pl.pallas_call(
        pad_kernel,
        grid=(slots,),
        out_shape=jax.ShapeDtypeStruct((slots, wide, wide), BF16),
        in_specs=[pl.BlockSpec((1, width, width), lambda s: (s, 0, 0))],
        out_specs=pl.BlockSpec((1, wide, wide), lambda s: (s, 0, 0)),
        cost_estimate=pl.CostEstimate(flops=slots * 4 * 10**9, bytes_accessed=7 * 10**6, transcendentals=0),
        compiler_params=pltpu.CompilerParams(vmem_limit_bytes=24 * MIB),
        name="pad_right_root",
    )(right_root[0, 0])
    tiles = (dp_count, mp_count, slots, row_part, LANES)
    arrived = exchange(outgoing).reshape(tiles)
    tile_spec = pl.BlockSpec((dp_count, mp_count, 1, row_part, LANES), lambda s, *_: (0, 0, s, 0, 0))
    leaving = pl.pallas_call(
        precond_kernel,
        grid=(slots,),
        out_shape=jax.ShapeDtypeStruct(tiles, BF16),
        in_specs=[
            tile_spec,
            pl.BlockSpec((1, width, width), lambda s: (s, 0, 0)),
            pl.BlockSpec((1, wide, wide), lambda s: (s, 0, 0)),
        ],
        out_specs=tile_spec,
        scratch_shapes=[pltpu.VMEM((width, wide), BF16)],
        cost_estimate=pl.CostEstimate(flops=slots * 3 * 10**9, bytes_accessed=13 * 10**6, transcendentals=0),
        compiler_params=pltpu.CompilerParams(vmem_limit_bytes=30 * MIB),
        name="precondition",
    )(arrived, left_root[0, 0], padded_root)
    returned = exchange(leaving.reshape(outgoing.shape))
    tile = width // 3
    stat_spec = pl.BlockSpec((1, tile, width), lambda s, i: (s, i, 0))
    left_new, right_new = pl.pallas_call(
        gram_kernel,
        grid=(slots, width // tile),
        out_shape=[jax.ShapeDtypeStruct((slots, width, width), F32)] * 2,
        in_specs=[tile_spec, stat_spec, stat_spec],
        out_specs=[stat_spec, stat_spec],
        scratch_shapes=[pltpu.VMEM((width, wide), BF16), pltpu.VMEM((width, width), BF16)],
        cost_estimate=pl.CostEstimate(flops=slots * 3 * 10**9, bytes_accessed=22 * 10**6, transcendentals=0),
        compiler_params=pltpu.CompilerParams(vmem_limit_bytes=30 * MIB),
        name="grams",
    )(arrived, left_stat[0, 0], right_stat[0, 0])
    precond = pl.pallas_call(
        unpack_kernel,
        out_shape=jax.ShapeDtypeStruct(gradient.shape, BF16),
        in_specs=[smem, vmem],
        out_specs=vmem,
        scratch_shapes=[rows_scratch, seen_scratch],
        compiler_params=pltpu.CompilerParams(vmem_limit_bytes=12 * MIB),
        name="unpack",
    )(owner, returned)
    return (precond, left_new[None, None], right_new[None, None])


def copy_in(src, dst, sem):
    copy = pltpu.make_async_copy(src, dst, sem)
    copy.start()
    return copy


def lane_of(shape):
    return lax.broadcasted_iota(jnp.int32, shape, len(shape) - 1)


def pack_pairs_kernel(
    owner_hbm, grad_hbm, out_hbm, table_hbm, bad_hbm, owner_ref, grad_ref, out_ref, rows_ref, table_ref, bad_ref, seen_ref, first_ref,
    pairs_ref, load_sems, store_sems, sems,
):
    row_blocks, row_part, col_blocks, col_part = grad_ref.shape
    devices, height = out_hbm.shape[:2]
    count = row_blocks * col_blocks
    tall = row_part * col_blocks
    chunks = load_sems.shape[0]
    span = row_blocks // chunks
    owner_copy = copy_in(owner_hbm, owner_ref, sems.at[0])
    copies = []
    for i in range(chunks):
        part = pl.ds(i * span, span)
        copies.append(copy_in(grad_hbm.at[part], grad_ref.at[part], load_sems.at[i]))
    me = lax.axis_index("dp") * lax.axis_size("mp") + lax.axis_index("mp")
    half = col_part // 2
    free = LANES - col_part
    rest = half - free
    groups = row_part // 8
    extras_at = devices
    info_at = 2 * devices

    def clear(i, carry):
        seen_ref[i] = 0
        pairs_ref[i] = 0
        first_ref[i] = count
        return carry

    lax.fori_loop(0, devices, clear, 0, unroll=8)
    rows_ref[pl.ds(row_blocks * tall, tall), :] = jnp.zeros((tall, LANES), F32)
    owner_copy.wait()

    def block_row(r, extras):
        rows_ref[pl.ds(r * tall, tall), col_part:] = jnp.zeros((tall, free), F32)
        rows_ref[pl.ds(r * tall, tall), :col_part] = grad_ref[r].astype(F32).reshape(tall, col_part)
        for c in range(col_blocks):
            block = r * col_blocks + c
            dest, slot = count_slots(owner_ref, seen_ref, block)
            table_ref[block] = jnp.where(slot == 0, dest, 0)
            first_ref[jnp.where(slot == 0, dest, devices)] = block
            table_ref[extras_at + extras] = block
            extras = extras + slot
        return extras

    extras = jnp.int32(0)
    for i in range(chunks):
        copies[i].wait()
        extras = lax.fori_loop(i * span, (i + 1) * span, block_row, extras)
    for i in range(3):
        table_ref[info_at + i] = 0
    table_ref[info_at + 3] = extras
    bad_ref[0] = 0

    def note(e, carry):
        dest = owner_ref[table_ref[extras_at + e]]
        pairs = pairs_ref[dest // 2]
        pairs_ref[dest // 2] = pairs + 1
        here = dest // 2 == me // 2
        table_ref[info_at] = jnp.where(here, 1, table_ref[info_at])
        table_ref[info_at + 1] = jnp.where(here, dest % 2, table_ref[info_at + 1])
        table_ref[info_at + 2] = jnp.where(dest == me, 1, table_ref[info_at + 2])
        bad_ref[0] = jnp.where(pairs > 0, 1, bad_ref[0])
        return carry

    lax.fori_loop(0, extras, note, 0)
    table_copy = copy_in(table_ref, table_hbm, sems.at[1])
    bad_copy = copy_in(bad_ref, bad_hbm, sems.at[2])

    def tile_of(block):
        return rows_ref[pl.ds(block // col_blocks * tall + block % col_blocks, row_part, stride=col_blocks), :]

    def message(d, carry):
        tile = tile_of(first_ref[d])
        out_ref[d] = jnp.concatenate([tile, jnp.zeros((height - row_part, LANES), F32)], axis=0).astype(BF16)
        return carry

    stores = []
    pieces = store_sems.shape[0]
    share = devices // pieces
    for i in range(pieces):
        lax.fori_loop(i * share, (i + 1) * share, message, 0, unroll=8)

        def extra(e, carry, i=i):
            block = table_ref[extras_at + e]
            chip = owner_ref[block] // 2

            @pl.when(2 * chip // share == i)
            def _():
                tile = tile_of(block)
                lane = lane_of((row_part, LANES))
                lane8 = lane_of((8, LANES))
                for j in range(2):
                    old = out_ref[2 * chip + j].astype(F32)
                    moved = pltpu.roll(tile, (col_part - half * j) % LANES, 1)
                    top = jnp.where(lane < col_part, old[:row_part], moved)
                    low = jnp.zeros((8, LANES), F32)
                    for k in range(groups):
                        piece = pltpu.roll(tile[8 * k : 8 * k + 8], (rest * k - half * j - free) % LANES, 1)
                        low = jnp.where(lane8 // rest == k, piece, low)
                    out_ref[2 * chip + j] = jnp.concatenate([top, low], axis=0).astype(BF16)

            return carry

        lax.fori_loop(0, extras, extra, 0)
        part = pl.ds(i * share, share)
        stores.append(copy_in(out_ref.at[part], out_hbm.at[part], store_sems.at[i]))
    table_copy.wait()
    bad_copy.wait()
    for store in stores:
        store.wait()


def unpack_pairs_kernel(owner_hbm, table_hbm, back_ref, out_hbm, owner_ref, table_ref, out_ref, rows_ref, sems, store_sems):
    row_blocks, row_part, col_blocks, col_part = out_ref.shape
    devices = back_ref.shape[0]
    owner_copy = copy_in(owner_hbm, owner_ref, sems.at[0])
    table_copy = copy_in(table_hbm, table_ref, sems.at[1])
    half = col_part // 2
    free = LANES - col_part
    rest = half - free
    groups = row_part // 8
    chunks = store_sems.shape[0]
    span = row_blocks // chunks
    owner_copy.wait()
    table_copy.wait()

    def finish(r, buffer):
        rows = rows_ref[buffer, :, :col_part].reshape(row_part, col_blocks, col_part)
        out_ref[r] = rows.astype(BF16)

    def block_row(r, buffer):
        for c in range(col_blocks):
            tile = back_ref[table_ref[r * col_blocks + c], :row_part, :]
            rows_ref[buffer, pl.ds(c, row_part, stride=col_blocks), :] = tile.astype(F32)
        finish(r, buffer)

    def body(t, carry):
        block_row(2 * t, 0)
        block_row(2 * t + 1, 1)
        return carry

    stores = []
    for i in range(chunks):
        lax.fori_loop(i * span // 2, (i + 1) * span // 2, body, 0)

        def extra(e, carry, i=i):
            block = table_ref[devices + e]
            chip = owner_ref[block] // 2
            r = block // col_blocks

            @pl.when(r // span == i)
            def _():
                lane = lane_of((row_part, LANES))
                tile = jnp.zeros((row_part, LANES), F32)
                for j in range(2):
                    message = back_ref[2 * chip + j].astype(F32)
                    top = pltpu.roll(message[:row_part], (half * j - col_part) % LANES, 1)
                    low = [
                        pltpu.roll(message[row_part : row_part + 8], (half * j + free - rest * k) % LANES, 1)
                        for k in range(groups)
                    ]
                    low = jnp.concatenate(low, axis=0)
                    tile = jnp.where((lane >= half * j) & (lane < half * j + free), top, tile)
                    tile = jnp.where((lane >= half * j + free) & (lane < half * j + half), low, tile)
                rows_ref[0, :, :col_part] = out_ref[r].astype(F32).reshape(row_part * col_blocks, col_part)
                rows_ref[0, pl.ds(block % col_blocks, row_part, stride=col_blocks), :] = tile
                finish(r, 0)

            return carry

        lax.fori_loop(0, table_ref[2 * devices + 3], extra, 0)
        part = pl.ds(i * span, span)
        stores.append(copy_in(out_ref.at[part], out_hbm.at[part], store_sems.at[i]))
    for store in stores:
        store.wait()


def halves_order(shape, core, axis, part, groups):
    half = part // 2
    free = LANES - part
    rest = half - free
    n = lax.broadcasted_iota(jnp.int32, shape, axis)
    tail = n - free * groups
    first = part * (n // free) + n % free
    second = part * (tail // rest) + free + tail % rest
    return half * core + jnp.where(tail < 0, first, second)


def swap_groups(rows, rest):
    rows = list(rows)
    count = len(rows)
    group = lane_of(rows[0].shape) // rest
    bit = 1
    while bit < count:
        low = group // bit % 2 == 0
        for i in range(count):
            if i // bit % 2 == 0:
                x, y = rows[i], rows[i + bit]
                rows[i] = jnp.where(low, x, pltpu.roll(y, rest * bit, 1))
                rows[i + bit] = jnp.where(low, pltpu.roll(x, LANES - rest * bit, 1), y)
        bit *= 2
    return rows


def prepare_kernel(
    table_ref, left_hbm, right_hbm, left_other_hbm, right_other_hbm, padded_ref, picked_ref, left0_ref, left1_ref, root_ref, root1_ref,
    sems,
):
    width = root_ref.shape[0]
    wide_all = padded_ref.shape[1]
    groups = wide_all // LANES
    part = width // groups
    half = width // 2
    free = LANES - part
    core = lax.axis_index("mp") % 2
    info_at = table_ref.shape[0] - LANES
    left0_copy = copy_in(left_hbm.at[0], left0_ref, sems.at[0])
    root_copy = copy_in(right_hbm.at[0], root_ref, sems.at[1])
    from_other = (table_ref[info_at] == 1) & (table_ref[info_at + 1] != core)

    @pl.when(from_other)
    def _():
        right = copy_in(right_other_hbm.at[1], root1_ref, sems.at[2])
        copy_in(left_other_hbm.at[1], left1_ref, sems.at[3]).wait()
        right.wait()

    @pl.when(jnp.logical_not(from_other))
    def _():
        right = copy_in(right_hbm.at[1], root1_ref, sems.at[2])
        copy_in(left_hbm.at[1], left1_ref, sems.at[3]).wait()
        right.wait()

    mine = jnp.where(
        halves_order((width, half), core, 1, part, groups) == lax.broadcasted_iota(jnp.int32, (width, half), 0), 1.0, 0.0
    ).astype(BF16)
    cols = jnp.dot(root1_ref[...], mine, preferred_element_type=F32).astype(BF16)
    for j in range(2):
        theirs = jnp.where(
            halves_order((half, width), j, 0, part, groups) == lax.broadcasted_iota(jnp.int32, (half, width), 1), 1.0, 0.0
        ).astype(BF16)
        picked_ref[j * half : (j + 1) * half, :] = jnp.dot(theirs, cols, preferred_element_type=F32).astype(BF16)
    root_copy.wait()
    spread = spread_matrix(part, LANES // (LANES - part))
    wide, narrow = spread.shape
    for g in range(width // narrow):
        rows = jnp.dot(spread, root_ref[g * narrow : (g + 1) * narrow, :], preferred_element_type=F32).astype(BF16)
        for h in range(width // narrow):
            cell = lax.dot_general(
                rows[:, h * narrow : (h + 1) * narrow], spread, (((1,), (1,)), ((), ())), preferred_element_type=F32
            )
            padded_ref[g * wide : (g + 1) * wide, h * wide : (h + 1) * wide] = cell.astype(BF16)
    row = lax.broadcasted_iota(jnp.int32, (free * groups, wide_all), 0)
    col = lax.broadcasted_iota(jnp.int32, (free * groups, wide_all), 1)
    hit = (col // LANES == row // free) & (col % LANES == part + row % free)
    padded_ref[wide_all:, :] = jnp.where(hit, 1.0, 0.0).astype(BF16)
    left0_copy.wait()


def take_matrix(part):
    free = LANES - part
    shape = ((LANES // free) * LANES, LANES)
    row = lax.broadcasted_iota(jnp.int32, shape, 0)
    col = lax.broadcasted_iota(jnp.int32, shape, 1)
    return jnp.where((row // LANES == col // free) & (row % LANES == part + col % free), 1.0, 0.0).astype(BF16)


def extract_kernel(arr_ref, roots_hbm, out_ref, tall_ref):
    row_groups, col_groups, height, _ = arr_ref.shape
    row_part = height - 8
    width = row_groups * row_part
    part = width // col_groups
    take = take_matrix(part)
    span = take.shape[0] // LANES
    for g in range(col_groups // span):
        tiles = [arr_ref[:, g * span + m, :row_part, :].reshape(width, LANES) for m in range(span)]
        cols = jnp.dot(jnp.concatenate(tiles, axis=1), take, preferred_element_type=F32)
        out_ref[:, g * LANES : (g + 1) * LANES] = cols.astype(BF16)
    low = [arr_ref[:, m, row_part:, :].astype(F32).reshape(8 * row_groups, LANES) for m in range(col_groups)]
    low = swap_groups(low, LANES // col_groups)
    for k in range(row_part // 8):
        tall_ref[:, k] = low[k].reshape(row_groups, 8, LANES)
    out_ref[:, width // 2 - LANES :] = tall_ref[...].reshape(width, LANES).astype(BF16)


def half_kernel(arr_ref, left_ref, half_ref, wide_hbm, wide_ref, sem):
    row_groups, col_groups, height, _ = arr_ref.shape
    row_part = height - 8
    for a in range(row_groups):
        for m in range(col_groups):
            wide_ref[a * row_part : (a + 1) * row_part, m * LANES : (m + 1) * LANES] = arr_ref[a, m, :row_part, :]
    wide_copy = copy_in(wide_ref, wide_hbm, sem)
    step = left_ref.shape[0] // 2
    for i in range(2):
        rows = slice(i * step, (i + 1) * step)
        half_ref[rows, :] = jnp.dot(left_ref[rows, :], wide_ref[...], preferred_element_type=F32).astype(BF16)
    wide_copy.wait()


def products_kernel(
    half_ref, right0_ref, mine_ref, other_ref, left1_ref, right1_ref, out_hbm, block_hbm, block_ref, message_ref, store_sems, block_sem,
):
    row_groups, col_groups, height, _ = message_ref.shape
    row_part = height - 8
    width = left1_ref.shape[0]
    half = width // 2
    groups = row_part // 8
    core = lax.axis_index("mp") % 2
    for j in range(2):

        @pl.when(core == j)
        def _(j=j):
            block_ref[:, j * half : (j + 1) * half] = mine_ref[...]
            block_ref[:, (1 - j) * half : (2 - j) * half] = other_ref[...]

    block_copy = copy_in(block_ref, block_hbm, block_sem)
    stores = []
    start = 0
    for i, span in enumerate(SPANS):
        rows = slice(start * row_part, (start + span) * row_part)
        temp = jnp.dot(left1_ref[rows, :], block_ref[...], preferred_element_type=F32).astype(BF16)
        extra = jnp.dot(temp, right1_ref[...], preferred_element_type=F32)
        both = jnp.concatenate([half_ref[rows, :], extra[:, : half - LANES].astype(BF16)], axis=1)
        result = jnp.dot(both, right0_ref[...], preferred_element_type=F32).astype(BF16)
        low = extra[:, half - LANES :].reshape(span, groups, 8, LANES)
        low = [low[:, k].reshape(8 * span, LANES) for k in range(groups)]
        low += [jnp.zeros((8 * span, LANES), F32)] * (col_groups - groups)
        low = swap_groups(low, LANES // col_groups)
        for k in range(span):
            for m in range(col_groups):
                message_ref[start + k, m, :row_part] = result[k * row_part : (k + 1) * row_part, m * LANES : (m + 1) * LANES]
                message_ref[start + k, m, row_part:] = low[m][8 * k : 8 * k + 8].astype(BF16)
        part = pl.ds(start, span)
        stores.append(copy_in(message_ref.at[part], out_hbm.at[part], store_sems.at[i]))
        start += span
    block_copy.wait()
    for store in stores:
        store.wait()


def pair_gram_kernel(table_ref, wide_ref, halves_ref, left_ref, right_ref, left_out, right_out, block_ref):
    width = block_ref.shape[0]
    col_groups = wide_ref.shape[1] // LANES
    part = width // col_groups
    tile = left_ref.shape[1]
    slot = pl.program_id(0)
    step = pl.program_id(1)
    has_extra = table_ref[table_ref.shape[0] - LANES + 2]

    @pl.when((step == 0) & (slot == 0))
    def _():
        spread = spread_matrix(part, LANES // (LANES - part))
        wide, narrow = spread.shape
        for g in range(width // narrow):
            cols = jnp.dot(wide_ref[:, g * wide : (g + 1) * wide], spread, preferred_element_type=F32)
            block_ref[:, g * narrow : (g + 1) * narrow] = cols.astype(BF16)

    @pl.when((step == 0) & (slot == 1) & (has_extra == 1))
    def _():
        half = width // 2
        total = jnp.zeros((width, width), F32)
        for j in range(2):
            order = halves_order((half, width), j, 0, part, col_groups)
            theirs = jnp.where(order == lax.broadcasted_iota(jnp.int32, (half, width), 1), 1.0, 0.0).astype(BF16)
            total += jnp.dot(halves_ref[:, j * half : (j + 1) * half], theirs, preferred_element_type=F32)
        block_ref[...] = total.astype(BF16)

    @pl.when((step == 0) & (slot == 1) & (has_extra == 0))
    def _():
        block_ref[...] = jnp.zeros_like(block_ref)

    for i in range(width // tile):

        @pl.when(step == i)
        def _(i=i):
            mine = slice(i * tile, (i + 1) * tile)
            left = lax.dot_general(
                block_ref[mine, :], block_ref[...], (((1,), (1,)), ((), ())), preferred_element_type=F32
            )
            left_out[0] = STAT_DECAY * left_ref[0] + (1.0 - STAT_DECAY) * left
            right = lax.dot_general(
                block_ref[:, mine], block_ref[...], (((0,), (0,)), ((), ())), preferred_element_type=F32
            )
            right_out[0] = STAT_DECAY * right_ref[0] + (1.0 - STAT_DECAY) * right


def exchange(x):
    return lax.all_to_all(x, ("dp", "mp"), split_axis=0, concat_axis=0, tiled=True)


def other_core(x):
    count = lax.axis_size("mp")
    return lax.ppermute(x, "mp", [(i, i ^ 1) for i in range(count)])


def pair_path(outgoing, table, gradient, owner, left_stat, right_stat, left_root, right_root):
    row_blocks, row_part, col_blocks, col_part = gradient.shape
    dp_count = lax.axis_size("dp")
    mp_count = lax.axis_size("mp")
    devices = dp_count * mp_count
    slots, width = left_stat.shape[2:4]
    wide = mp_count * LANES
    height = outgoing.shape[1]
    groups = row_part // 8
    pieces = 4
    smem = pl.BlockSpec(memory_space=pltpu.SMEM)
    vmem = pl.BlockSpec(memory_space=pltpu.VMEM)
    hbm = pl.BlockSpec(memory_space=HBM)
    anywhere = pl.BlockSpec(memory_space=pl.ANY)
    dma = pltpu.SemaphoreType.DMA
    message_shape = (dp_count, mp_count, height, LANES)
    left_root = left_root[0, 0]
    right_root = right_root[0, 0]

    def params(mib):
        return pltpu.CompilerParams(vmem_limit_bytes=mib * MIB)

    def cost(flops, moved):
        return pl.CostEstimate(flops=int(flops * 1e9), bytes_accessed=int(moved * 1e6), transcendentals=0)

    def in_hbm(x):
        return pltpu.with_memory_space_constraint(x, HBM)

    arrived = exchange(outgoing).reshape(message_shape)
    padded, picked, left0, left1 = pl.pallas_call(
        prepare_kernel,
        out_shape=[
            HBM((wide + mp_count * (LANES - col_part), wide), BF16),
            HBM((width, width // 2), BF16),
            HBM((width, width), BF16),
            HBM((width, width), BF16),
        ],
        in_specs=[smem, hbm, hbm, hbm, hbm],
        out_specs=[vmem] * 4,
        scratch_shapes=[pltpu.VMEM((width, width), BF16), pltpu.VMEM((width, width), BF16), dma((4,))],
        cost_estimate=cost(6, 9),
        compiler_params=params(24),
        name="prepare_roots",
    )(table, left_root, right_root, other_core(left_root), other_core(right_root))
    mine = pl.pallas_call(
        extract_kernel,
        out_shape=jax.ShapeDtypeStruct((width, width // 2), BF16),
        in_specs=[vmem, hbm],
        out_specs=vmem,
        scratch_shapes=[pltpu.VMEM((dp_count, groups, 8, LANES), F32)],
        cost_estimate=cost(0.6, 3),
        compiler_params=params(16),
        name="extract_extra",
    )(arrived, in_hbm(left1))
    other = other_core(mine)
    half, block = pl.pallas_call(
        half_kernel,
        out_shape=[pltpu.VMEM((width, wide), BF16), HBM((width, wide), BF16)],
        in_specs=[vmem, vmem],
        out_specs=[vmem, hbm],
        scratch_shapes=[pltpu.VMEM((width, wide), BF16), dma],
        cost_estimate=cost(2, 6),
        compiler_params=params(16),
        name="half_product",
    )(arrived, left0)
    leaving, halves = pl.pallas_call(
        products_kernel,
        out_shape=[HBM(message_shape, BF16), HBM((width, width), BF16)],
        in_specs=[vmem] * 6,
        out_specs=[hbm] * 2,
        scratch_shapes=[
            pltpu.VMEM((width, width), BF16),
            pltpu.VMEM(message_shape, BF16),
            dma((len(SPANS),)),
            dma,
        ],
        cost_estimate=cost(5, 12),
        compiler_params=params(28),
        name="precondition",
    )(half, padded, mine, other, left1, picked)
    returned = exchange(leaving.reshape(outgoing.shape))
    tile = width // 3
    stat_spec = pl.BlockSpec((1, tile, width), lambda s, i: (s, i, 0))
    left_new, right_new = pl.pallas_call(
        pair_gram_kernel,
        grid=(slots, width // tile),
        out_shape=[jax.ShapeDtypeStruct((slots, width, width), F32)] * 2,
        in_specs=[
            smem,
            pl.BlockSpec((width, wide), lambda s, i: (0, 0)),
            pl.BlockSpec((width, width), lambda s, i: (0, 0)),
            stat_spec,
            stat_spec,
        ],
        out_specs=[stat_spec, stat_spec],
        scratch_shapes=[pltpu.VMEM((width, width), BF16)],
        cost_estimate=cost(9, 25),
        compiler_params=params(24),
        name="pair_grams",
    )(table, in_hbm(block), in_hbm(halves), left_stat[0, 0], right_stat[0, 0])
    precond = pl.pallas_call(
        unpack_pairs_kernel,
        out_shape=HBM(gradient.shape, BF16),
        in_specs=[anywhere, anywhere, vmem],
        out_specs=hbm,
        scratch_shapes=[
            pltpu.SMEM(owner.shape, jnp.int32),
            pltpu.SMEM(table.shape, jnp.int32),
            pltpu.VMEM(gradient.shape, BF16),
            pltpu.VMEM((2, row_part * col_blocks, LANES), F32),
            dma((2,)),
            dma((pieces,)),
        ],
        compiler_params=params(12),
        name="unpack_pairs",
    )(owner, table, returned)
    return (precond, left_new[None, None], right_new[None, None])


def per_device(gradient, owner, left_stat, right_stat, left_root, right_root):
    row_blocks, row_part, col_blocks, col_part = gradient.shape
    devices = lax.axis_size("dp") * lax.axis_size("mp")
    height = row_part + 8
    hbm = pl.BlockSpec(memory_space=HBM)
    dma = pltpu.SemaphoreType.DMA
    outgoing, table, bad = pl.pallas_call(
        pack_pairs_kernel,
        out_shape=[
            HBM((devices, height, LANES), BF16),
            HBM((2 * devices + LANES,), jnp.int32),
            HBM((LANES,), jnp.int32),
        ],
        in_specs=[hbm, hbm],
        out_specs=[hbm, hbm, hbm],
        scratch_shapes=[
            pltpu.SMEM(owner.shape, jnp.int32),
            pltpu.VMEM(gradient.shape, BF16),
            pltpu.VMEM((devices, height, LANES), BF16),
            pltpu.VMEM(((row_blocks + 1) * row_part * col_blocks, LANES), F32),
            pltpu.SMEM((2 * devices + LANES,), jnp.int32),
            pltpu.SMEM((LANES,), jnp.int32),
            pltpu.SMEM((devices,), jnp.int32),
            pltpu.SMEM((devices + 1,), jnp.int32),
            pltpu.SMEM((devices,), jnp.int32),
            dma((2,)),
            dma((4,)),
            dma((3,)),
        ],
        compiler_params=pltpu.CompilerParams(vmem_limit_bytes=16 * MIB),
        name="pack_pairs",
    )(owner, gradient)
    rest = (gradient, owner, left_stat, right_stat, left_root, right_root)
    if not FALLBACK:
        return pair_path(outgoing, table, *rest)
    return lax.cond(bad[0] == 0, pair_path, lambda outgoing, table, *rest: general_path(*rest), outgoing, table, *rest)


def solution(mesh):
    return jax.shard_map(
        per_device,
        mesh=mesh,
        in_specs=(
            P(None, "dp", None, "mp"),
            P(),
            P("dp", "mp", None, None, None),
            P("dp", "mp", None, None, None),
            P("dp", "mp", None, None, None),
            P("dp", "mp", None, None, None),
        ),
        out_specs=(
            P(None, "dp", None, "mp"),
            P("dp", "mp", None, None, None),
            P("dp", "mp", None, None, None),
        ),
        check_vma=False,
    )
```

```python
import jax
import jax.numpy as jnp
from jax import lax
from jax.experimental import pallas as pl
from jax.experimental.pallas import tpu as pltpu
from jax.sharding import PartitionSpec as P

STAT_DECAY = 0.98
LANES = 128
F32 = jnp.float32
BF16 = jnp.bfloat16
MIB = 1024 * 1024
FALLBACK = True
HBM = pltpu.HBM
SPANS = (8, 4, 4)


def spread_matrix(part, groups):
    row = lax.broadcasted_iota(jnp.int32, (groups * LANES, groups * part), 0)
    col = lax.broadcasted_iota(jnp.int32, (groups * LANES, groups * part), 1)
    hit = (row // LANES == col // part) & (row % LANES == col % part)
    return jnp.where(hit, 1.0, 0.0).astype(BF16)


def count_slots(owner_ref, seen_ref, block):
    dest = owner_ref[block]
    slot = seen_ref[dest]
    seen_ref[dest] = slot + 1
    return dest, slot


def clear_counts(seen_ref, devices):
    def clear(i, carry):
        seen_ref[i] = 0
        return carry

    lax.fori_loop(0, devices, clear, 0)


def pack_kernel(owner_ref, grad_ref, out_ref, rows_ref, seen_ref):
    row_blocks, row_part, col_blocks, col_part = grad_ref.shape
    devices, slots = out_ref.shape[:2]
    clear_counts(seen_ref, devices)
    rows_ref[...] = jnp.zeros_like(rows_ref)

    def clear(i, carry):
        for s in range(slots):
            out_ref[i, s] = jnp.zeros((row_part, LANES), BF16)
        return carry

    lax.fori_loop(0, devices, clear, 0)

    def block_row(r, carry):
        rows_ref[:, :col_part] = grad_ref[r].astype(F32).reshape(row_part * col_blocks, col_part)
        for c in range(col_blocks):
            dest, slot = count_slots(owner_ref, seen_ref, r * col_blocks + c)
            tile = rows_ref[pl.ds(c, row_part, stride=col_blocks), :]
            out_ref[dest, slot] = tile.astype(BF16)
        return carry

    lax.fori_loop(0, row_blocks, block_row, 0)


def unpack_kernel(owner_ref, back_ref, out_ref, rows_ref, seen_ref):
    row_blocks, row_part, col_blocks, col_part = out_ref.shape
    devices = back_ref.shape[0]
    clear_counts(seen_ref, devices)

    def block_row(r, carry):
        for c in range(col_blocks):
            dest, slot = count_slots(owner_ref, seen_ref, r * col_blocks + c)
            rows_ref[pl.ds(c, row_part, stride=col_blocks), :] = back_ref[dest, slot].astype(F32)
        rows = rows_ref[:, :col_part].reshape(row_part, col_blocks, col_part)
        out_ref[r] = rows.astype(BF16)
        return carry

    lax.fori_loop(0, row_blocks, block_row, 0)


def pad_kernel(root_ref, out_ref):
    width = root_ref.shape[1]
    part = width // (out_ref.shape[1] // LANES)
    groups = LANES // (LANES - part)
    spread = spread_matrix(part, groups)
    wide, narrow = spread.shape
    for g in range(width // narrow):
        rows = jnp.dot(spread, root_ref[0, g * narrow : (g + 1) * narrow, :], preferred_element_type=F32).astype(BF16)
        for h in range(width // narrow):
            cell = lax.dot_general(
                rows[:, h * narrow : (h + 1) * narrow], spread, (((1,), (1,)), ((), ())), preferred_element_type=F32
            )
            out_ref[0, g * wide : (g + 1) * wide, h * wide : (h + 1) * wide] = cell.astype(BF16)


def gather_tiles(arr_ref, wide_ref):
    row_groups, col_groups, _, row_part, _ = arr_ref.shape
    for a in range(row_groups):
        for m in range(col_groups):
            wide_ref[a * row_part : (a + 1) * row_part, m * LANES : (m + 1) * LANES] = arr_ref[a, m, 0]


def precond_kernel(arr_ref, left_ref, right_ref, out_ref, wide_ref):
    row_groups, col_groups, _, row_part, _ = arr_ref.shape
    gather_tiles(arr_ref, wide_ref)
    step = 4 * row_part
    for i in range(row_groups // 4):
        half = jnp.dot(left_ref[0, i * step : (i + 1) * step, :], wide_ref[...], preferred_element_type=F32).astype(BF16)
        result = jnp.dot(half, right_ref[0], preferred_element_type=F32).astype(BF16)
        for k in range(4):
            for m in range(col_groups):
                out_ref[4 * i + k, m, 0] = result[k * row_part : (k + 1) * row_part, m * LANES : (m + 1) * LANES]


def gram_kernel(arr_ref, left_ref, right_ref, left_out, right_out, wide_ref, block_ref):
    width = block_ref.shape[0]
    part = width // arr_ref.shape[1]
    tile = left_ref.shape[1]
    step = pl.program_id(1)

    @pl.when(step == 0)
    def _():
        gather_tiles(arr_ref, wide_ref)
        spread = spread_matrix(part, LANES // (LANES - part))
        wide, narrow = spread.shape
        for g in range(width // narrow):
            cols = jnp.dot(wide_ref[:, g * wide : (g + 1) * wide], spread, preferred_element_type=F32)
            block_ref[:, g * narrow : (g + 1) * narrow] = cols.astype(BF16)

    for i in range(width // tile):

        @pl.when(step == i)
        def _(i=i):
            mine = slice(i * tile, (i + 1) * tile)
            left = lax.dot_general(
                block_ref[mine, :], block_ref[...], (((1,), (1,)), ((), ())), preferred_element_type=F32
            )
            left_out[0] = STAT_DECAY * left_ref[0] + (1.0 - STAT_DECAY) * left
            right = lax.dot_general(
                block_ref[:, mine], block_ref[...], (((0,), (0,)), ((), ())), preferred_element_type=F32
            )
            right_out[0] = STAT_DECAY * right_ref[0] + (1.0 - STAT_DECAY) * right


def general_path(gradient, owner, left_stat, right_stat, left_root, right_root):
    row_blocks, row_part, col_blocks, col_part = gradient.shape
    dp_count = lax.axis_size("dp")
    mp_count = lax.axis_size("mp")
    devices = dp_count * mp_count
    slots, width = left_stat.shape[2:4]
    wide = mp_count * LANES
    smem = pl.BlockSpec(memory_space=pltpu.SMEM)
    vmem = pl.BlockSpec(memory_space=pltpu.VMEM)
    rows_scratch = pltpu.VMEM((row_part * col_blocks, LANES), F32)
    seen_scratch = pltpu.SMEM((devices,), jnp.int32)

    def exchange(x):
        return lax.all_to_all(x, ("dp", "mp"), split_axis=0, concat_axis=0, tiled=True)

    outgoing = pl.pallas_call(
        pack_kernel,
        out_shape=jax.ShapeDtypeStruct((devices, slots, row_part, LANES), BF16),
        in_specs=[smem, vmem],
        out_specs=vmem,
        scratch_shapes=[rows_scratch, seen_scratch],
        compiler_params=pltpu.CompilerParams(vmem_limit_bytes=12 * MIB),
        name="pack",
    )(owner, gradient)
    padded_root = pl.pallas_call(
        pad_kernel,
        grid=(slots,),
        out_shape=jax.ShapeDtypeStruct((slots, wide, wide), BF16),
        in_specs=[pl.BlockSpec((1, width, width), lambda s: (s, 0, 0))],
        out_specs=pl.BlockSpec((1, wide, wide), lambda s: (s, 0, 0)),
        cost_estimate=pl.CostEstimate(flops=slots * 4 * 10**9, bytes_accessed=7 * 10**6, transcendentals=0),
        compiler_params=pltpu.CompilerParams(vmem_limit_bytes=24 * MIB),
        name="pad_right_root",
    )(right_root[0, 0])
    tiles = (dp_count, mp_count, slots, row_part, LANES)
    arrived = exchange(outgoing).reshape(tiles)
    tile_spec = pl.BlockSpec((dp_count, mp_count, 1, row_part, LANES), lambda s, *_: (0, 0, s, 0, 0))
    leaving = pl.pallas_call(
        precond_kernel,
        grid=(slots,),
        out_shape=jax.ShapeDtypeStruct(tiles, BF16),
        in_specs=[
            tile_spec,
            pl.BlockSpec((1, width, width), lambda s: (s, 0, 0)),
            pl.BlockSpec((1, wide, wide), lambda s: (s, 0, 0)),
        ],
        out_specs=tile_spec,
        scratch_shapes=[pltpu.VMEM((width, wide), BF16)],
        cost_estimate=pl.CostEstimate(flops=slots * 3 * 10**9, bytes_accessed=13 * 10**6, transcendentals=0),
        compiler_params=pltpu.CompilerParams(vmem_limit_bytes=30 * MIB),
        name="precondition",
    )(arrived, left_root[0, 0], padded_root)
    returned = exchange(leaving.reshape(outgoing.shape))
    tile = width // 3
    stat_spec = pl.BlockSpec((1, tile, width), lambda s, i: (s, i, 0))
    left_new, right_new = pl.pallas_call(
        gram_kernel,
        grid=(slots, width // tile),
        out_shape=[jax.ShapeDtypeStruct((slots, width, width), F32)] * 2,
        in_specs=[tile_spec, stat_spec, stat_spec],
        out_specs=[stat_spec, stat_spec],
        scratch_shapes=[pltpu.VMEM((width, wide), BF16), pltpu.VMEM((width, width), BF16)],
        cost_estimate=pl.CostEstimate(flops=slots * 3 * 10**9, bytes_accessed=22 * 10**6, transcendentals=0),
        compiler_params=pltpu.CompilerParams(vmem_limit_bytes=30 * MIB),
        name="grams",
    )(arrived, left_stat[0, 0], right_stat[0, 0])
    precond = pl.pallas_call(
        unpack_kernel,
        out_shape=jax.ShapeDtypeStruct(gradient.shape, BF16),
        in_specs=[smem, vmem],
        out_specs=vmem,
        scratch_shapes=[rows_scratch, seen_scratch],
        compiler_params=pltpu.CompilerParams(vmem_limit_bytes=12 * MIB),
        name="unpack",
    )(owner, returned)
    return (precond, left_new[None, None], right_new[None, None])


def copy_in(src, dst, sem):
    copy = pltpu.make_async_copy(src, dst, sem)
    copy.start()
    return copy


def lane_of(shape):
    return lax.broadcasted_iota(jnp.int32, shape, len(shape) - 1)


def pack_pairs_kernel(
    owner_hbm, grad_hbm, out_hbm, table_hbm, bad_hbm, owner_ref, grad_ref, out_ref, rows_ref, table_ref, bad_ref, seen_ref, first_ref,
    pairs_ref, load_sems, store_sems, sems,
):
    row_blocks, row_part, col_blocks, col_part = grad_ref.shape
    devices, height = out_hbm.shape[:2]
    count = row_blocks * col_blocks
    tall = row_part * col_blocks
    chunks = load_sems.shape[0]
    span = row_blocks // chunks
    owner_copy = copy_in(owner_hbm, owner_ref, sems.at[0])
    copies = []
    for i in range(chunks):
        part = pl.ds(i * span, span)
        copies.append(copy_in(grad_hbm.at[part], grad_ref.at[part], load_sems.at[i]))
    me = lax.axis_index("dp") * lax.axis_size("mp") + lax.axis_index("mp")
    half = col_part // 2
    free = LANES - col_part
    rest = half - free
    groups = row_part // 8
    extras_at = devices
    info_at = 2 * devices

    def clear(i, carry):
        seen_ref[i] = 0
        pairs_ref[i] = 0
        first_ref[i] = count
        return carry

    lax.fori_loop(0, devices, clear, 0, unroll=8)
    rows_ref[pl.ds(row_blocks * tall, tall), :] = jnp.zeros((tall, LANES), F32)
    owner_copy.wait()

    def block_row(r, extras):
        rows_ref[pl.ds(r * tall, tall), col_part:] = jnp.zeros((tall, free), F32)
        rows_ref[pl.ds(r * tall, tall), :col_part] = grad_ref[r].astype(F32).reshape(tall, col_part)
        for c in range(col_blocks):
            block = r * col_blocks + c
            dest, slot = count_slots(owner_ref, seen_ref, block)
            table_ref[block] = jnp.where(slot == 0, dest, 0)
            first_ref[jnp.where(slot == 0, dest, devices)] = block
            table_ref[extras_at + extras] = block
            extras = extras + slot
        return extras

    extras = jnp.int32(0)
    for i in range(chunks):
        copies[i].wait()
        extras = lax.fori_loop(i * span, (i + 1) * span, block_row, extras)
    for i in range(3):
        table_ref[info_at + i] = 0
    table_ref[info_at + 3] = extras
    bad_ref[0] = 0

    def note(e, carry):
        dest = owner_ref[table_ref[extras_at + e]]
        pairs = pairs_ref[dest // 2]
        pairs_ref[dest // 2] = pairs + 1
        here = dest // 2 == me // 2
        table_ref[info_at] = jnp.where(here, 1, table_ref[info_at])
        table_ref[info_at + 1] = jnp.where(here, dest % 2, table_ref[info_at + 1])
        table_ref[info_at + 2] = jnp.where(dest == me, 1, table_ref[info_at + 2])
        bad_ref[0] = jnp.where(pairs > 0, 1, bad_ref[0])
        return carry

    lax.fori_loop(0, extras, note, 0)
    table_copy = copy_in(table_ref, table_hbm, sems.at[1])
    bad_copy = copy_in(bad_ref, bad_hbm, sems.at[2])

    def tile_of(block):
        return rows_ref[pl.ds(block // col_blocks * tall + block % col_blocks, row_part, stride=col_blocks), :]

    def message(d, carry):
        tile = tile_of(first_ref[d])
        out_ref[d] = jnp.concatenate([tile, jnp.zeros((height - row_part, LANES), F32)], axis=0).astype(BF16)
        return carry

    pieces = store_sems.shape[0]
    share = devices // pieces

    def store(i):
        part = pl.ds(i * share, share)
        return pltpu.make_async_copy(out_ref.at[part], out_hbm.at[part], store_sems.at[i])

    def piece(i, carry):
        lax.fori_loop(0, share, lambda d, carry: message(i * share + d, carry), 0, unroll=8)

        def extra(e, carry):
            block = table_ref[extras_at + e]
            chip = owner_ref[block] // 2

            @pl.when(2 * chip // share == i)
            def _():
                tile = tile_of(block)
                lane = lane_of((row_part, LANES))
                lane8 = lane_of((8, LANES))
                for j in range(2):
                    old = out_ref[2 * chip + j].astype(F32)
                    moved = pltpu.roll(tile, (col_part - half * j) % LANES, 1)
                    top = jnp.where(lane < col_part, old[:row_part], moved)
                    low = jnp.zeros((8, LANES), F32)
                    for k in range(groups):
                        piece = pltpu.roll(tile[8 * k : 8 * k + 8], (rest * k - half * j - free) % LANES, 1)
                        low = jnp.where(lane8 // rest == k, piece, low)
                    out_ref[2 * chip + j] = jnp.concatenate([top, low], axis=0).astype(BF16)

            return carry

        lax.fori_loop(0, extras, extra, 0)
        store(i).start()
        return carry

    lax.fori_loop(0, pieces, piece, 0)
    table_copy.wait()
    bad_copy.wait()
    for i in range(pieces):
        store(i).wait()


def unpack_pairs_kernel(owner_hbm, table_hbm, back_ref, out_hbm, owner_ref, table_ref, out_ref, rows_ref, sems, store_sems):
    row_blocks, row_part, col_blocks, col_part = out_ref.shape
    devices = back_ref.shape[0]
    owner_copy = copy_in(owner_hbm, owner_ref, sems.at[0])
    table_copy = copy_in(table_hbm, table_ref, sems.at[1])
    half = col_part // 2
    free = LANES - col_part
    rest = half - free
    groups = row_part // 8
    chunks = store_sems.shape[0]
    span = row_blocks // chunks
    owner_copy.wait()
    table_copy.wait()

    def finish(r, buffer):
        rows = rows_ref[buffer, :, :col_part].reshape(row_part, col_blocks, col_part)
        out_ref[r] = rows.astype(BF16)

    def block_row(r, buffer):
        for c in range(col_blocks):
            tile = back_ref[table_ref[r * col_blocks + c], :row_part, :]
            rows_ref[buffer, pl.ds(c, row_part, stride=col_blocks), :] = tile.astype(F32)
        finish(r, buffer)

    def body(t, carry):
        block_row(2 * t, 0)
        block_row(2 * t + 1, 1)
        return carry

    def store(i):
        part = pl.ds(i * span, span)
        return pltpu.make_async_copy(out_ref.at[part], out_hbm.at[part], store_sems.at[i])

    def piece(i, carry):
        lax.fori_loop(0, span // 2, lambda t, carry: body(i * (span // 2) + t, carry), 0)

        def extra(e, carry):
            block = table_ref[devices + e]
            chip = owner_ref[block] // 2
            r = block // col_blocks

            @pl.when(r // span == i)
            def _():
                lane = lane_of((row_part, LANES))
                tile = jnp.zeros((row_part, LANES), F32)
                for j in range(2):
                    message = back_ref[2 * chip + j].astype(F32)
                    top = pltpu.roll(message[:row_part], (half * j - col_part) % LANES, 1)
                    low = [
                        pltpu.roll(message[row_part : row_part + 8], (half * j + free - rest * k) % LANES, 1)
                        for k in range(groups)
                    ]
                    low = jnp.concatenate(low, axis=0)
                    tile = jnp.where((lane >= half * j) & (lane < half * j + free), top, tile)
                    tile = jnp.where((lane >= half * j + free) & (lane < half * j + half), low, tile)
                rows_ref[0, :, :col_part] = out_ref[r].astype(F32).reshape(row_part * col_blocks, col_part)
                rows_ref[0, pl.ds(block % col_blocks, row_part, stride=col_blocks), :] = tile
                finish(r, 0)

            return carry

        lax.fori_loop(0, table_ref[2 * devices + 3], extra, 0)
        store(i).start()
        return carry

    lax.fori_loop(0, chunks, piece, 0)
    for i in range(chunks):
        store(i).wait()


def halves_order(shape, core, axis, part, groups):
    half = part // 2
    free = LANES - part
    rest = half - free
    n = lax.broadcasted_iota(jnp.int32, shape, axis)
    tail = n - free * groups
    first = part * (n // free) + n % free
    second = part * (tail // rest) + free + tail % rest
    return half * core + jnp.where(tail < 0, first, second)


def swap_groups(rows, rest):
    rows = list(rows)
    count = len(rows)
    group = lane_of(rows[0].shape) // rest
    bit = 1
    while bit < count:
        low = group // bit % 2 == 0
        for i in range(count):
            if i // bit % 2 == 0:
                x, y = rows[i], rows[i + bit]
                rows[i] = jnp.where(low, x, pltpu.roll(y, rest * bit, 1))
                rows[i + bit] = jnp.where(low, pltpu.roll(x, LANES - rest * bit, 1), y)
        bit *= 2
    return rows


def prepare_kernel(
    table_ref, left_hbm, right_hbm, left_other_hbm, right_other_hbm, padded_ref, picked_ref, left0_ref, left1_ref, root_ref, root1_ref,
    sems,
):
    width = root_ref.shape[0]
    wide_all = padded_ref.shape[1]
    groups = wide_all // LANES
    part = width // groups
    half = width // 2
    free = LANES - part
    core = lax.axis_index("mp") % 2
    info_at = table_ref.shape[0] - LANES
    left0_copy = copy_in(left_hbm.at[0], left0_ref, sems.at[0])
    root_copy = copy_in(right_hbm.at[0], root_ref, sems.at[1])
    from_other = (table_ref[info_at] == 1) & (table_ref[info_at + 1] != core)

    @pl.when(from_other)
    def _():
        right = copy_in(right_other_hbm.at[1], root1_ref, sems.at[2])
        copy_in(left_other_hbm.at[1], left1_ref, sems.at[3]).wait()
        right.wait()

    @pl.when(jnp.logical_not(from_other))
    def _():
        right = copy_in(right_hbm.at[1], root1_ref, sems.at[2])
        copy_in(left_hbm.at[1], left1_ref, sems.at[3]).wait()
        right.wait()

    mine = jnp.where(
        halves_order((width, half), core, 1, part, groups) == lax.broadcasted_iota(jnp.int32, (width, half), 0), 1.0, 0.0
    ).astype(BF16)
    cols = jnp.dot(root1_ref[...], mine, preferred_element_type=F32).astype(BF16)
    for j in range(2):
        theirs = jnp.where(
            halves_order((half, width), j, 0, part, groups) == lax.broadcasted_iota(jnp.int32, (half, width), 1), 1.0, 0.0
        ).astype(BF16)
        picked_ref[j * half : (j + 1) * half, :] = jnp.dot(theirs, cols, preferred_element_type=F32).astype(BF16)
    root_copy.wait()
    spread = spread_matrix(part, LANES // (LANES - part))
    wide, narrow = spread.shape
    for g in range(width // narrow):
        rows = jnp.dot(spread, root_ref[g * narrow : (g + 1) * narrow, :], preferred_element_type=F32).astype(BF16)
        for h in range(width // narrow):
            cell = lax.dot_general(
                rows[:, h * narrow : (h + 1) * narrow], spread, (((1,), (1,)), ((), ())), preferred_element_type=F32
            )
            padded_ref[g * wide : (g + 1) * wide, h * wide : (h + 1) * wide] = cell.astype(BF16)
    row = lax.broadcasted_iota(jnp.int32, (free * groups, wide_all), 0)
    col = lax.broadcasted_iota(jnp.int32, (free * groups, wide_all), 1)
    hit = (col // LANES == row // free) & (col % LANES == part + row % free)
    padded_ref[wide_all:, :] = jnp.where(hit, 1.0, 0.0).astype(BF16)
    left0_copy.wait()


def take_matrix(part):
    free = LANES - part
    shape = ((LANES // free) * LANES, LANES)
    row = lax.broadcasted_iota(jnp.int32, shape, 0)
    col = lax.broadcasted_iota(jnp.int32, shape, 1)
    return jnp.where((row // LANES == col // free) & (row % LANES == part + col % free), 1.0, 0.0).astype(BF16)


def extract_kernel(arr_ref, roots_hbm, out_ref, tall_ref):
    row_groups, col_groups, height, _ = arr_ref.shape
    row_part = height - 8
    width = row_groups * row_part
    part = width // col_groups
    take = take_matrix(part)
    span = take.shape[0] // LANES
    for g in range(col_groups // span):
        tiles = [arr_ref[:, g * span + m, :row_part, :].reshape(width, LANES) for m in range(span)]
        cols = jnp.dot(jnp.concatenate(tiles, axis=1), take, preferred_element_type=F32)
        out_ref[:, g * LANES : (g + 1) * LANES] = cols.astype(BF16)
    low = [arr_ref[:, m, row_part:, :].astype(F32).reshape(8 * row_groups, LANES) for m in range(col_groups)]
    low = swap_groups(low, LANES // col_groups)
    for k in range(row_part // 8):
        tall_ref[:, k] = low[k].reshape(row_groups, 8, LANES)
    out_ref[:, width // 2 - LANES :] = tall_ref[...].reshape(width, LANES).astype(BF16)


def half_kernel(arr_ref, left_ref, half_ref, wide_hbm, wide_ref, sem):
    row_groups, col_groups, height, _ = arr_ref.shape
    row_part = height - 8
    for a in range(row_groups):
        for m in range(col_groups):
            wide_ref[a * row_part : (a + 1) * row_part, m * LANES : (m + 1) * LANES] = arr_ref[a, m, :row_part, :]
    wide_copy = copy_in(wide_ref, wide_hbm, sem)
    step = left_ref.shape[0] // 2
    for i in range(2):
        rows = slice(i * step, (i + 1) * step)
        half_ref[rows, :] = jnp.dot(left_ref[rows, :], wide_ref[...], preferred_element_type=F32).astype(BF16)
    wide_copy.wait()


def products_kernel(
    half_ref, right0_ref, mine_ref, other_ref, left1_ref, right1_ref, out_hbm, block_hbm, block_ref, message_ref, store_sems, block_sem,
):
    row_groups, col_groups, height, _ = message_ref.shape
    row_part = height - 8
    width = left1_ref.shape[0]
    half = width // 2
    groups = row_part // 8
    core = lax.axis_index("mp") % 2
    for j in range(2):

        @pl.when(core == j)
        def _(j=j):
            block_ref[:, j * half : (j + 1) * half] = mine_ref[...]
            block_ref[:, (1 - j) * half : (2 - j) * half] = other_ref[...]

    block_copy = copy_in(block_ref, block_hbm, block_sem)
    stores = []
    start = 0
    for i, span in enumerate(SPANS):
        rows = slice(start * row_part, (start + span) * row_part)
        temp = jnp.dot(left1_ref[rows, :], block_ref[...], preferred_element_type=F32).astype(BF16)
        extra = jnp.dot(temp, right1_ref[...], preferred_element_type=F32)
        both = jnp.concatenate([half_ref[rows, :], extra[:, : half - LANES].astype(BF16)], axis=1)
        result = jnp.dot(both, right0_ref[...], preferred_element_type=F32).astype(BF16)
        low = extra[:, half - LANES :].reshape(span, groups, 8, LANES)
        low = [low[:, k].reshape(8 * span, LANES) for k in range(groups)]
        low += [jnp.zeros((8 * span, LANES), F32)] * (col_groups - groups)
        low = swap_groups(low, LANES // col_groups)
        for k in range(span):
            for m in range(col_groups):
                message_ref[start + k, m, :row_part] = result[k * row_part : (k + 1) * row_part, m * LANES : (m + 1) * LANES]
                message_ref[start + k, m, row_part:] = low[m][8 * k : 8 * k + 8].astype(BF16)
        part = pl.ds(start, span)
        stores.append(copy_in(message_ref.at[part], out_hbm.at[part], store_sems.at[i]))
        start += span
    block_copy.wait()
    for store in stores:
        store.wait()


def pair_gram_kernel(table_ref, wide_ref, halves_ref, left_ref, right_ref, left_out, right_out, block_ref):
    width = block_ref.shape[0]
    col_groups = wide_ref.shape[1] // LANES
    part = width // col_groups
    tile = left_ref.shape[1]
    slot = pl.program_id(0)
    step = pl.program_id(1)
    has_extra = table_ref[table_ref.shape[0] - LANES + 2]

    @pl.when((step == 0) & (slot == 0))
    def _():
        spread = spread_matrix(part, LANES // (LANES - part))
        wide, narrow = spread.shape
        for g in range(width // narrow):
            cols = jnp.dot(wide_ref[:, g * wide : (g + 1) * wide], spread, preferred_element_type=F32)
            block_ref[:, g * narrow : (g + 1) * narrow] = cols.astype(BF16)

    @pl.when((step == 0) & (slot == 1) & (has_extra == 1))
    def _():
        half = width // 2
        total = jnp.zeros((width, width), F32)
        for j in range(2):
            order = halves_order((half, width), j, 0, part, col_groups)
            theirs = jnp.where(order == lax.broadcasted_iota(jnp.int32, (half, width), 1), 1.0, 0.0).astype(BF16)
            total += jnp.dot(halves_ref[:, j * half : (j + 1) * half], theirs, preferred_element_type=F32)
        block_ref[...] = total.astype(BF16)

    @pl.when((step == 0) & (slot == 1) & (has_extra == 0))
    def _():
        block_ref[...] = jnp.zeros_like(block_ref)

    for i in range(width // tile):

        @pl.when(step == i)
        def _(i=i):
            mine = slice(i * tile, (i + 1) * tile)
            left = lax.dot_general(
                block_ref[mine, :], block_ref[...], (((1,), (1,)), ((), ())), preferred_element_type=F32
            )
            left_out[0] = STAT_DECAY * left_ref[0] + (1.0 - STAT_DECAY) * left
            right = lax.dot_general(
                block_ref[:, mine], block_ref[...], (((0,), (0,)), ((), ())), preferred_element_type=F32
            )
            right_out[0] = STAT_DECAY * right_ref[0] + (1.0 - STAT_DECAY) * right


def exchange(x):
    return lax.all_to_all(x, ("dp", "mp"), split_axis=0, concat_axis=0, tiled=True)


def other_core(x):
    count = lax.axis_size("mp")
    return lax.ppermute(x, "mp", [(i, i ^ 1) for i in range(count)])


def pair_path(outgoing, table, gradient, owner, left_stat, right_stat, left_root, right_root):
    row_blocks, row_part, col_blocks, col_part = gradient.shape
    dp_count = lax.axis_size("dp")
    mp_count = lax.axis_size("mp")
    devices = dp_count * mp_count
    slots, width = left_stat.shape[2:4]
    wide = mp_count * LANES
    height = outgoing.shape[1]
    groups = row_part // 8
    pieces = 4
    smem = pl.BlockSpec(memory_space=pltpu.SMEM)
    vmem = pl.BlockSpec(memory_space=pltpu.VMEM)
    hbm = pl.BlockSpec(memory_space=HBM)
    anywhere = pl.BlockSpec(memory_space=pl.ANY)
    dma = pltpu.SemaphoreType.DMA
    message_shape = (dp_count, mp_count, height, LANES)
    left_root = left_root[0, 0]
    right_root = right_root[0, 0]

    def params(mib):
        return pltpu.CompilerParams(vmem_limit_bytes=mib * MIB)

    def cost(flops, moved):
        return pl.CostEstimate(flops=int(flops * 1e9), bytes_accessed=int(moved * 1e6), transcendentals=0)

    def in_hbm(x):
        return pltpu.with_memory_space_constraint(x, HBM)

    arrived = exchange(outgoing).reshape(message_shape)
    padded, picked, left0, left1 = pl.pallas_call(
        prepare_kernel,
        out_shape=[
            HBM((wide + mp_count * (LANES - col_part), wide), BF16),
            HBM((width, width // 2), BF16),
            HBM((width, width), BF16),
            HBM((width, width), BF16),
        ],
        in_specs=[smem, hbm, hbm, hbm, hbm],
        out_specs=[vmem] * 4,
        scratch_shapes=[pltpu.VMEM((width, width), BF16), pltpu.VMEM((width, width), BF16), dma((4,))],
        cost_estimate=cost(6, 9),
        compiler_params=params(24),
        name="prepare_roots",
    )(table, left_root, right_root, other_core(left_root), other_core(right_root))
    mine = pl.pallas_call(
        extract_kernel,
        out_shape=jax.ShapeDtypeStruct((width, width // 2), BF16),
        in_specs=[vmem, hbm],
        out_specs=vmem,
        scratch_shapes=[pltpu.VMEM((dp_count, groups, 8, LANES), F32)],
        cost_estimate=cost(0.6, 3),
        compiler_params=params(16),
        name="extract_extra",
    )(arrived, in_hbm(left1))
    other = other_core(mine)
    half, block = pl.pallas_call(
        half_kernel,
        out_shape=[pltpu.VMEM((width, wide), BF16), HBM((width, wide), BF16)],
        in_specs=[vmem, vmem],
        out_specs=[vmem, hbm],
        scratch_shapes=[pltpu.VMEM((width, wide), BF16), dma],
        cost_estimate=cost(2, 6),
        compiler_params=params(16),
        name="half_product",
    )(arrived, left0)
    leaving, halves = pl.pallas_call(
        products_kernel,
        out_shape=[HBM(message_shape, BF16), HBM((width, width), BF16)],
        in_specs=[vmem] * 6,
        out_specs=[hbm] * 2,
        scratch_shapes=[
            pltpu.VMEM((width, width), BF16),
            pltpu.VMEM(message_shape, BF16),
            dma((len(SPANS),)),
            dma,
        ],
        cost_estimate=cost(5, 12),
        compiler_params=params(28),
        name="precondition",
    )(half, padded, mine, other, left1, picked)
    returned = exchange(leaving.reshape(outgoing.shape))
    tile = width // 3
    stat_spec = pl.BlockSpec((1, tile, width), lambda s, i: (s, i, 0))
    left_new, right_new = pl.pallas_call(
        pair_gram_kernel,
        grid=(slots, width // tile),
        out_shape=[jax.ShapeDtypeStruct((slots, width, width), F32)] * 2,
        in_specs=[
            smem,
            pl.BlockSpec((width, wide), lambda s, i: (0, 0)),
            pl.BlockSpec((width, width), lambda s, i: (0, 0)),
            stat_spec,
            stat_spec,
        ],
        out_specs=[stat_spec, stat_spec],
        scratch_shapes=[pltpu.VMEM((width, width), BF16)],
        cost_estimate=cost(9, 25),
        compiler_params=params(24),
        name="pair_grams",
    )(table, in_hbm(block), in_hbm(halves), left_stat[0, 0], right_stat[0, 0])
    precond = pl.pallas_call(
        unpack_pairs_kernel,
        out_shape=HBM(gradient.shape, BF16),
        in_specs=[anywhere, anywhere, vmem],
        out_specs=hbm,
        scratch_shapes=[
            pltpu.SMEM(owner.shape, jnp.int32),
            pltpu.SMEM(table.shape, jnp.int32),
            pltpu.VMEM(gradient.shape, BF16),
            pltpu.VMEM((2, row_part * col_blocks, LANES), F32),
            dma((2,)),
            dma((pieces,)),
        ],
        compiler_params=params(12),
        name="unpack_pairs",
    )(owner, table, returned)
    return (precond, left_new[None, None], right_new[None, None])


def per_device(gradient, owner, left_stat, right_stat, left_root, right_root):
    row_blocks, row_part, col_blocks, col_part = gradient.shape
    devices = lax.axis_size("dp") * lax.axis_size("mp")
    height = row_part + 8
    hbm = pl.BlockSpec(memory_space=HBM)
    dma = pltpu.SemaphoreType.DMA
    outgoing, table, bad = pl.pallas_call(
        pack_pairs_kernel,
        out_shape=[
            HBM((devices, height, LANES), BF16),
            HBM((2 * devices + LANES,), jnp.int32),
            HBM((LANES,), jnp.int32),
        ],
        in_specs=[hbm, hbm],
        out_specs=[hbm, hbm, hbm],
        scratch_shapes=[
            pltpu.SMEM(owner.shape, jnp.int32),
            pltpu.VMEM(gradient.shape, BF16),
            pltpu.VMEM((devices, height, LANES), BF16),
            pltpu.VMEM(((row_blocks + 1) * row_part * col_blocks, LANES), F32),
            pltpu.SMEM((2 * devices + LANES,), jnp.int32),
            pltpu.SMEM((LANES,), jnp.int32),
            pltpu.SMEM((devices,), jnp.int32),
            pltpu.SMEM((devices + 1,), jnp.int32),
            pltpu.SMEM((devices,), jnp.int32),
            dma((2,)),
            dma((4,)),
            dma((3,)),
        ],
        compiler_params=pltpu.CompilerParams(vmem_limit_bytes=16 * MIB),
        name="pack_pairs",
    )(owner, gradient)
    rest = (gradient, owner, left_stat, right_stat, left_root, right_root)
    if not FALLBACK:
        return pair_path(outgoing, table, *rest)
    return lax.cond(bad[0] == 0, pair_path, lambda outgoing, table, *rest: general_path(*rest), outgoing, table, *rest)


def solution(mesh):
    return jax.shard_map(
        per_device,
        mesh=mesh,
        in_specs=(
            P(None, "dp", None, "mp"),
            P(),
            P("dp", "mp", None, None, None),
            P("dp", "mp", None, None, None),
            P("dp", "mp", None, None, None),
            P("dp", "mp", None, None, None),
        ),
        out_specs=(
            P(None, "dp", None, "mp"),
            P("dp", "mp", None, None, None),
            P("dp", "mp", None, None, None),
        ),
        check_vma=False,
    )
```
